32 devices in a mesh: basin: 8 (over z, y), member: 4 (over x, core).
Axes of the slice: x: 2, y: 2, z: 4, core: 2. Of those that a mesh axis runs over, the one named last changes fastest.
Arguments:
- forcing: bfloat16 [512, 16, 192], P('basin', 'member'), may hold values from -6 to 6
- tile_part: int32 [512, 2], P('basin'), may hold values from 0 to 7, all different within a row; in each aligned block of 64 rows (0 to 63, 64 to 127, ...) at most 32 rows name the same one
- tile_slot: int32 [512, 2], P('basin'), may hold values from 0 to 31
- tile_weight: float32 [512, 2], P('basin'), may hold values from 0.2 to 1
- w_input: bfloat16 [8, 1024], replicated, may hold values from -2 to 2
- w_encoder: bfloat16 [256, 1024], replicated, may hold values from -0.375 to 0.375
- b_encoder: float32 [1024], replicated, may hold values from -3 to 3
- w_decoder: bfloat16 [256, 1024], replicated, may hold values from -0.375 to 0.375
- b_decoder: float32 [1024], replicated, may hold values from -3 to 3
- w_output: bfloat16 [256], replicated, may hold values from -0.75 to 0.75
- celerity: float32 [256], replicated, may hold values from 0.5 to 4
- storage: float32 [256], replicated, may hold values from 0.5 to 2
- initial_flow: float32 [256, 16], P('basin', 'member'), may hold values from 0.5 to 2
- reach_level: int32 [256], replicated, may hold values from 0 to 3
- upstream: int32 [256, 4], replicated, may hold values from -1 to 255, as said below
Outputs:
- discharge: float32 [256, 16, 6], P('basin', 'member')
- ensemble_mean: float32 [256, 6], P('basin')
The draws below stay inside these ranges and needn't reach their ends.
Inputs may be any that keep to these rules, and one draw needn't show every extreme that they name: `tile_part`: among the tile rows of one index of basin, no partition is named more than 32 times. `upstream`: each entry is -1 or the index of a reach whose level is lower than this reach's level; reaches of level 0 have only -1.
All inputs are finite; a program needn't handle non-finite values.
Results may differ from the reference program's by a relative error of at most 0.0003.
Values may be sent and summed in bfloat16 or wider, within the bound.
No kernel may reach another device: no remote copies, remote signals or barrier semaphores. Data moves between devices by JAX's collectives and lax.ppermute only.
A program may use at most 192 MiB of HBM per device.

```python
import math
import jax
import jax.numpy as jnp
import numpy as np
from jax import lax

UNITS = 256
FEAT = 8
ENC = 24
DEC = 6
TOP = 2
UPS = 4
LEVELS = 4
NEWTON = 4
BAS_DEV = 32
TILE_DEV = 64
PARTS_SIZE = 8
CAP = 32
BASINS = 256
TILES = 512
MEMBERS = 16


def topology_draw(key):
    level_key = jax.random.fold_in(key, 11)
    link_key = jax.random.fold_in(key, 23)
    levels_all = jax.random.randint(level_key, (BASINS,), 0, LEVELS).astype(jnp.int32)
    candidate = jax.random.randint(link_key, (BASINS, UPS), 0, BASINS).astype(jnp.int32)
    valid = levels_all[candidate] < levels_all[:, None]
    linked = jnp.where(valid, candidate, -1).astype(jnp.int32)
    return (levels_all, linked)


def draw_reach_level(key, part):
    return topology_draw(key)[0]


def draw_upstream(key, part):
    return topology_draw(key)[1]


def touch_ends(values, stream_key, least, largest):
    extent = values.shape
    spot = [jax.random.randint(jax.random.fold_in(stream_key, axis), (), 0, extent[axis]) for axis in range(len(extent))]
    values = values.at[tuple(spot)].set(least)
    longest = extent.index(max(extent))
    spot[longest] = (spot[longest] + 1) % extent[longest]
    return values.at[tuple(spot)].set(largest)


def block_scale(stream_key, extent, pieces, smallest, largest):
    def one(dim, shards_of):
        heights = jax.random.uniform(jax.random.fold_in(jax.random.fold_in(stream_key, 6), dim), (shards_of,), jnp.float32, smallest / len(pieces), largest / len(pieces))
        return jnp.repeat(jnp.exp(heights), extent[dim] // shards_of).reshape((-1,) + (1,) * (len(extent) - dim - 1))

    factor_of = one(*pieces[0])
    for cut in pieces[1:]:
        factor_of = factor_of * one(*cut)
    return factor_of


def shared_out(key, own, number, rows, amount, top, reach, lean):
    sequence = jax.random.permutation(key, amount)
    heavy_load, common = load_shares(amount, rows * top, reach, lean, True), load_shares(amount, rows * top, reach, lean, False)
    places = jnp.arange(amount)

    def named(sizes, turn):
        used = int((sizes > 0).sum())
        fixed = max(1, used // 4)
        passed = fixed + (places - fixed + turn * (used - fixed)) % max(1, amount - fixed)
        return jnp.zeros((amount,), jnp.int32).at[sequence[jnp.where(places < fixed, places, passed)]].set(jnp.asarray(sizes, jnp.int32))

    sizes = jnp.where(number % 4 == 0, named(heavy_load, number // 4), named(common, number - number // 4 - 1))
    mixed = jax.random.permutation(jax.random.fold_in(own, 3), amount)
    source_of, taker = mixed[0:amount // 2 * 2:2], mixed[1:amount // 2 * 2:2]
    margin = jnp.minimum(sizes[source_of] - 1, reach - sizes[taker]) // 2
    margin = jnp.where((source_of == sequence[0]) | (taker == sequence[0]) | (sizes[taker] == 0), 0, jnp.maximum(margin, 0))
    passed = jax.random.randint(jax.random.fold_in(own, 4), (amount // 2,), 0, 1 << 20) % (margin + 1)
    sizes = sizes.at[source_of].add(-passed).at[taker].add(passed)
    labels = jnp.searchsorted(jnp.cumsum(sizes), jnp.arange(rows * top), side="right").astype(jnp.int32)
    listing = labels.reshape(top, rows).T
    listing = listing[jax.random.permutation(jax.random.fold_in(own, 1), rows)]
    turn = jax.random.randint(jax.random.fold_in(own, 2), (rows, 1), 0, top)
    return jnp.take_along_axis(listing, (jnp.arange(top)[None, :] + turn) % top, axis=1)


def load_shares(number_of, total, limit, slope, full):
    portions = [(1 << 20) // math.isqrt(rank ** slope) + 1 for rank in range(1, number_of + 1)]
    largest = limit if full else min(limit, max(-(-total // number_of), total * portions[0] // sum(portions)))
    least = 1 if total - largest >= number_of - 1 else 0
    given, rest = [largest] + [least] * (number_of - 1), total - largest - least * (number_of - 1)
    while rest > 0:
        movable = [i for i in range(1, number_of) if given[i] < largest] or [i for i in range(1, number_of) if given[i] < limit]
        whole, budget = sum([portions[i] for i in movable]), rest
        for i in movable:
            addition = min(limit - given[i], max(1, budget * portions[i] // whole), rest)
            given[i] = given[i] + addition
            rest = rest - addition
    return np.array(given)


def bell_draw(stream_key, dims, deviation, most, split=(), kind=jnp.bfloat16):
    entries = deviation * jax.random.normal(stream_key, dims, jnp.float32)
    if split:
        entries = entries * block_scale(stream_key, dims, split, -0.22, 0.18)
    return jnp.clip(entries, -most, most).astype(kind)


def setup_inputs(seed: int = 0) -> dict:
    streams_of = jax.random.split(jax.random.key(seed), 16)
    forcing = bell_draw(streams_of[0], (TILES, MEMBERS, ENC * FEAT), 1.0, 6.0, ((0, 8), (1, 4)))
    tile_part_keys = jax.random.split(jax.random.fold_in(streams_of[1], 1), TILES // TILE_DEV)
    tile_part_turns = jax.random.permutation(jax.random.fold_in(streams_of[1], 3), TILES // TILE_DEV)
    tile_part = jax.vmap(lambda own, number: shared_out(jax.random.fold_in(streams_of[1], 2), own, number, TILE_DEV, PARTS_SIZE, TOP, CAP, 1))(tile_part_keys, tile_part_turns).reshape((TILES, TOP))
    tile_slot = touch_ends(jax.random.randint(streams_of[2], (TILES, TOP), 0, BAS_DEV), jax.random.fold_in(streams_of[2], 1), 0, BAS_DEV - 1).astype(jnp.int32)
    tile_weight = jnp.clip(0.2 + 0.8 * jax.random.uniform(streams_of[3], (TILES, TOP), jnp.float32) ** block_scale(streams_of[3], (TILES, TOP), ((0, 8),), -0.2, 0.2), 0.2, 1.0)
    w_input = bell_draw(streams_of[4], (FEAT, 4 * UNITS), FEAT ** -0.5, 2.0)
    w_encoder = bell_draw(streams_of[5], (UNITS, 4 * UNITS), UNITS ** -0.5, 0.375)
    b_encoder = bell_draw(streams_of[6], (4 * UNITS,), 0.5, 3.0, (), jnp.float32)
    w_decoder = bell_draw(streams_of[7], (UNITS, 4 * UNITS), UNITS ** -0.5, 0.375)
    b_decoder = bell_draw(streams_of[8], (4 * UNITS,), 0.5, 3.0, (), jnp.float32)
    w_output = bell_draw(streams_of[9], (UNITS,), (UNITS // 4) ** -0.5, 0.75)
    celerity = jnp.clip(jnp.exp(jax.random.uniform(streams_of[10], (BASINS,), jnp.float32, math.log(0.5), math.log(4.0))), 0.5, 4.0)
    storage = jnp.clip(jnp.exp(jax.random.uniform(streams_of[11], (BASINS,), jnp.float32, math.log(0.5), math.log(2.0))), 0.5, 2.0)
    initial_flow = jnp.clip(jnp.exp(math.log(2.0) - 1.3862944 * jax.random.uniform(streams_of[12], (BASINS, MEMBERS), jnp.float32) ** block_scale(streams_of[12], (BASINS, MEMBERS), ((0, 8), (1, 4)), -0.2, 0.2)), 0.5, 2.0)
    reach_level = draw_reach_level(jax.random.fold_in(streams_of[15], 71), 0)
    upstream = draw_upstream(jax.random.fold_in(streams_of[15], 71), 0)
    return {"forcing": forcing, "tile_part": tile_part, "tile_slot": tile_slot, "tile_weight": tile_weight, "w_input": w_input, "w_encoder": w_encoder, "b_encoder": b_encoder, "w_decoder": w_decoder, "b_decoder": b_decoder, "w_output": w_output, "celerity": celerity, "storage": storage, "initial_flow": initial_flow, "reach_level": reach_level, "upstream": upstream}


BETA = 0.6


def cell_update(gate_sum, memory_cell):
    unit_count = memory_cell.shape[-1]
    input_gate = jax.nn.sigmoid(gate_sum[:, :unit_count])
    forget_gate = jax.nn.sigmoid(gate_sum[:, unit_count:2 * unit_count])
    candidate = jnp.tanh(gate_sum[:, 2 * unit_count:3 * unit_count])
    output_gate = jax.nn.sigmoid(gate_sum[:, 3 * unit_count:])
    memory_cell = forget_gate * memory_cell + input_gate * candidate
    hidden = (output_gate * jnp.tanh(memory_cell)).astype(jnp.bfloat16)
    return hidden, memory_cell


def run_lstm(inputs, w_input, w_encoder, b_encoder, w_decoder, b_decoder, w_output):
    row_count = inputs.shape[0]
    unit_count = w_encoder.shape[0]
    hidden = jnp.zeros((row_count, unit_count), jnp.bfloat16)
    memory_cell = jnp.zeros((row_count, unit_count), jnp.float32)

    def encode(state_pair, forcing_hour):
        hidden, memory_cell = state_pair
        gate_sum = jnp.dot(forcing_hour, w_input, preferred_element_type=jnp.float32)
        gate_sum = gate_sum + jnp.dot(hidden, w_encoder, preferred_element_type=jnp.float32) + b_encoder
        return cell_update(gate_sum, memory_cell), None

    (hidden, memory_cell), ignored = lax.scan(encode, (hidden, memory_cell), jnp.swapaxes(inputs, 0, 1))

    def decode(state_pair, unused):
        hidden, memory_cell = state_pair
        gate_sum = jnp.dot(hidden, w_decoder, preferred_element_type=jnp.float32) + b_decoder
        hidden, memory_cell = cell_update(gate_sum, memory_cell)
        runoff = jax.nn.softplus(jnp.dot(hidden, w_output, preferred_element_type=jnp.float32))
        return (hidden, memory_cell), runoff

    ignored, runoff = lax.scan(decode, (hidden, memory_cell), None, length=DEC)
    return jnp.swapaxes(runoff, 0, 1)


def route_level(source, upstream, celerity, storage, lateral, initial):
    padded = jnp.concatenate([source, jnp.zeros((1,) + source.shape[1:], source.dtype)], axis=0)
    up_index = jnp.where(upstream < 0, source.shape[0], upstream).astype(jnp.int32)
    inflow = padded[up_index[:, 0]]
    for entry in range(1, up_index.shape[1]):
        inflow = inflow + padded[up_index[:, entry]]
    speed_rate = celerity[:, None]
    store_rate = storage[:, None]
    previous = initial
    series = []
    for hour_index in range(lateral.shape[2]):
        target = speed_rate * inflow[:, :, hour_index] + store_rate * previous ** BETA + lateral[:, :, hour_index]
        current = previous
        for newton_step in range(NEWTON):
            misfit = speed_rate * current + store_rate * current ** BETA - target
            slope_value = speed_rate + BETA * store_rate * current ** (BETA - 1.0)
            current = jnp.maximum(current - misfit / slope_value, 0.5 * current)
        series.append(current)
        previous = current
    return jnp.stack(series, axis=2)


def reference(forcing, tile_part, tile_slot, tile_weight, w_input, w_encoder, b_encoder, w_decoder, b_decoder, w_output, celerity, storage, initial_flow, reach_level, upstream):
    tile_count = forcing.shape[0]
    weighted = (tile_weight[:, :, None, None] * forcing[:, None, :, :].astype(jnp.float32)).astype(jnp.bfloat16)
    flat_terms = weighted.reshape(tile_count * TOP, -1).astype(jnp.float32)
    basin_ids = (tile_part * BAS_DEV + tile_slot).reshape(-1).astype(jnp.int32)
    aggregated = jax.ops.segment_sum(flat_terms, basin_ids, num_segments=BASINS)
    inputs = aggregated.astype(jnp.bfloat16).reshape(BASINS * MEMBERS, ENC, FEAT)
    lateral = run_lstm(inputs, w_input, w_encoder, b_encoder, w_decoder, b_decoder, w_output)
    lateral = lateral.reshape(BASINS, MEMBERS, DEC)
    outflow = jnp.zeros((BASINS, MEMBERS, DEC), jnp.float32)
    for level_now in range(LEVELS):
        routed = route_level(outflow, upstream, celerity, storage, lateral, initial_flow)
        outflow = jnp.where((reach_level == level_now)[:, None, None], routed, outflow)
    ensemble = jnp.sum(outflow, axis=1) / MEMBERS
    return outflow, ensemble
```

```python
import functools

import jax
import jax.numpy as jnp
from jax import lax
from jax.experimental import pallas as pl
from jax.experimental.pallas import tpu as pltpu
from jax.sharding import PartitionSpec as P

FEAT = 8
DEC = 6
TOP = 2
LEVELS = 4
NEWTON = 4
BETA = 0.6
LANES = 128
KERNEL_REACHES = 512

dot = functools.partial(jnp.dot, preferred_element_type=jnp.float32)


def three_pieces(values):
    high = lax.reduce_precision(values, 8, 7)
    rest = values - high
    middle = lax.reduce_precision(rest, 8, 7)
    return [high, middle, rest - middle]


def cell_update(gate_sum, memory_cell):
    units = memory_cell.shape[-1]
    input_gate = 0.5 * jnp.tanh(0.5 * gate_sum[:, :units]) + 0.5
    forget_gate = 0.5 * jnp.tanh(0.5 * gate_sum[:, units : 2 * units]) + 0.5
    candidate = jnp.tanh(gate_sum[:, 2 * units : 3 * units])
    output_gate = 0.5 * jnp.tanh(0.5 * gate_sum[:, 3 * units :]) + 0.5
    memory_cell = forget_gate * memory_cell + input_gate * candidate
    hidden = (output_gate * jnp.tanh(memory_cell)).astype(jnp.bfloat16)
    return hidden, memory_cell


def lstm_kernel(
    shape, arrived, w_input, w_encoder, b_encoder, w_decoder, b_decoder, w_output, out
):
    hour_feat, basin_local, groups, sources = shape
    hours = hour_feat // FEAT
    devices, tile_local, _ = arrived.shape
    rows = out.shape[1]
    units = w_encoder.shape[0]
    half = lax.rem(lax.axis_index("basin"), groups)
    first = half * rows
    extra_at = hour_feat // LANES * LANES
    lane0 = hour_feat - extra_at

    def add_sources(chunk, total):
        block = arrived[pl.ds(chunk * sources, sources)]
        block = block.reshape(sources * tile_local, block.shape[2]).astype(jnp.float32)
        extra = block[:, extra_at : extra_at + LANES]
        across = extra.T
        for entry in range(TOP):
            col = lane0 + 3 * entry
            weight = extra[:, col : col + 1] + extra[:, col + 1 : col + 2] + extra[:, col + 2 : col + 3]
            term = (weight * block).astype(jnp.bfloat16)
            part = lane0 + 3 * TOP + entry
            slot = part + TOP
            basin = across[part : part + 1] * basin_local + across[slot : slot + 1]
            basin = basin.astype(jnp.int32) - first
            row_of = lax.broadcasted_iota(jnp.int32, (rows, sources * tile_local), 0)
            picked = jnp.where(row_of == basin, 1.0, 0.0).astype(jnp.bfloat16)
            total = total + dot(picked, term)
        return total

    total = jnp.zeros((rows, arrived.shape[2]), jnp.float32)
    if devices == sources:
        total = add_sources(0, total)
    else:
        total = lax.fori_loop(0, devices // sources, add_sources, total)
    inputs = total.astype(jnp.bfloat16)

    owners = rows // basin_local
    flow = arrived[pl.ds(half * owners, owners), 0:basin_local, extra_at : extra_at + LANES]
    flow = flow.astype(jnp.float32).reshape(rows, LANES).T
    at = lane0 + 5 * TOP
    flow = flow[at : at + 1] + flow[at + 1 : at + 2] + flow[at + 2 : at + 3]
    out[DEC : DEC + 1, :] = flow
    out[DEC + 1 :, :] = jnp.zeros((out.shape[0] - DEC - 1, rows), jnp.float32)

    hidden = jnp.zeros((rows, units), jnp.bfloat16)
    memory_cell = jnp.zeros((rows, units), jnp.float32)
    for hour in range(hours):
        gate_sum = dot(inputs[:, hour * FEAT : (hour + 1) * FEAT], w_input[...]) + b_encoder[...]
        gate_sum = gate_sum + dot(hidden, w_encoder[...])
        hidden, memory_cell = cell_update(gate_sum, memory_cell)
    for hour in range(DEC):
        gate_sum = dot(hidden, w_decoder[...]) + b_decoder[...]
        hidden, memory_cell = cell_update(gate_sum, memory_cell)
        runoff = lax.dot_general(
            w_output[...], hidden, (((1,), (1,)), ((), ())), preferred_element_type=jnp.float32
        )[0:1]
        runoff = jnp.maximum(runoff, 0.0) + jnp.log(1.0 + jnp.exp(-jnp.abs(runoff)))
        out[hour : hour + 1, :] = runoff


def power(flow):
    return jnp.exp(BETA * jnp.log(flow))


def route_kernel(member_local, basin_local, gathered, upstream, level_row, celerity, storage, discharge, ensemble):
    reaches = level_row.shape[1]
    halves = reaches // LANES
    per_member = halves * 8
    members = gathered.shape[0] // per_member
    levels = jnp.broadcast_to(level_row[...], (members, reaches))
    source = lax.broadcasted_iota(jnp.int32, (reaches, reaches), 0)
    links = jnp.zeros((reaches, reaches), jnp.float32)
    for entry in range(upstream.shape[0]):
        links = links + jnp.where(source == upstream[entry : entry + 1, :], 1.0, 0.0)
    links = links.astype(jnp.bfloat16)
    speed_rate = jnp.broadcast_to(celerity[...], (members, reaches))
    store_rate = jnp.broadcast_to(storage[...], (members, reaches))

    def row(k):
        return jnp.concatenate(
            [gathered[pl.ds(h * 8 + k, members, stride=per_member), :] for h in range(halves)], axis=1
        )

    lateral = [row(k) for k in range(DEC)]
    current = row(DEC)
    powered = power(current)
    series = [jnp.zeros((members, reaches), jnp.float32) for _ in range(DEC)]
    for step in range(DEC + LEVELS - 1):
        target = jnp.zeros((members, reaches), jnp.float32)
        parts, owners = [], []
        for level in range(LEVELS):
            hour = step - level
            if 0 <= hour < DEC:
                target = jnp.where(levels == level, lateral[hour], target)
                if level:
                    flow = series[hour]
                    for _ in range(3):
                        piece = flow.astype(jnp.bfloat16)
                        parts.append(piece)
                        flow = flow - piece.astype(jnp.float32)
                    owners.append(level)
        if parts:
            sums = dot(jnp.concatenate(parts, axis=0), links)
            for i, level in enumerate(owners):
                at = 3 * i * members
                inflow = sums[at : at + members] + sums[at + members : at + 2 * members]
                inflow = inflow + sums[at + 2 * members : at + 3 * members]
                target = jnp.where(levels == level, target + speed_rate * inflow, target)
        target = target + store_rate * powered
        flow, flow_power = current, powered
        for _ in range(NEWTON):
            ratio = (target - (1.0 - BETA) * store_rate * flow_power) / (
                speed_rate * flow + BETA * store_rate * flow_power
            )
            flow = flow * jnp.maximum(ratio, 0.5)
            flow_power = power(flow)
        active = (levels <= step) & (levels > step - DEC)
        current = jnp.where(active, flow, current)
        powered = jnp.where(active, flow_power, powered)
        for level in range(LEVELS):
            hour = step - level
            if 0 <= hour < DEC:
                series[hour] = jnp.where(levels == level, flow, series[hour])
    column = lax.axis_index("basin") * basin_local
    mine = lax.axis_index("member")
    block = column // LANES
    shift = lax.rem(LANES - lax.rem(column, LANES), LANES)
    for hour in range(DEC):
        value = series[hour]
        picked = value[:, 0:LANES]
        for h in range(1, halves):
            picked = jnp.where(block == h, value[:, h * LANES : (h + 1) * LANES], picked)
        picked = pltpu.roll(picked, shift, 1)
        kept = picked[0:member_local]
        for q in range(1, members // member_local):
            kept = jnp.where(mine == q, picked[q * member_local : (q + 1) * member_local], kept)
        discharge[hour] = kept[:, 0:basin_local]
        mean = jnp.sum(picked, axis=0, keepdims=True) / members
        ensemble[hour : hour + 1, :] = mean[:, 0:basin_local]


def route_plain(gathered, upstream, reach_level, celerity, storage, mem_local, basin_local):
    reaches = reach_level.shape[0]
    members = gathered.shape[0] * gathered.shape[2] // reaches
    whole = gathered.reshape(members, -1, gathered.shape[1], gathered.shape[2])
    whole = jnp.transpose(whole, (1, 3, 0, 2)).reshape(reaches, members, gathered.shape[1])
    lateral, initial = whole[:, :, :DEC], whole[:, :, DEC]
    speed_rate, store_rate = celerity[:, None], storage[:, None]
    up_index = jnp.where(upstream < 0, reaches, upstream)
    outflow = jnp.zeros_like(lateral)
    for level_now in range(LEVELS):
        padded = jnp.concatenate([outflow, jnp.zeros_like(outflow[:1])], axis=0)
        inflow = padded[up_index[:, 0]]
        for entry in range(1, up_index.shape[1]):
            inflow = inflow + padded[up_index[:, entry]]
        flow = initial
        hours = []
        for hour in range(DEC):
            flow_power = flow**BETA
            target = speed_rate * inflow[:, :, hour] + store_rate * flow_power + lateral[:, :, hour]
            for _ in range(NEWTON):
                flow_power = flow**BETA
                ratio = (target - (1.0 - BETA) * store_rate * flow_power) / (
                    speed_rate * flow + BETA * store_rate * flow_power
                )
                flow = flow * jnp.maximum(ratio, 0.5)
            hours.append(flow)
        routed = jnp.stack(hours, axis=2)
        outflow = jnp.where((reach_level == level_now)[:, None, None], routed, outflow)
    ensemble = jnp.sum(outflow, axis=1) / members
    first_row = lax.axis_index("basin") * basin_local
    mine = lax.dynamic_slice_in_dim(outflow, first_row, basin_local, 0)
    mine = lax.dynamic_slice_in_dim(mine, lax.axis_index("member") * mem_local, mem_local, 1)
    return mine, lax.dynamic_slice_in_dim(ensemble, first_row, basin_local, 0)


def on_device(
    forcing,
    tile_part,
    tile_slot,
    tile_weight,
    w_input,
    w_encoder,
    b_encoder,
    w_decoder,
    b_decoder,
    w_output,
    celerity,
    storage,
    initial_flow,
    reach_level,
    upstream,
):
    tile_local, mem_local, hour_feat = forcing.shape
    part_count = lax.axis_size("basin")
    basin_local = initial_flow.shape[0]
    reaches = reach_level.shape[0]
    groups = part_count // mem_local
    rows = reaches // groups
    width = -(-(hour_feat + 5 * TOP + 3) // LANES) * LANES

    weight_pieces = three_pieces(tile_weight)
    columns = [piece[:, entry] for entry in range(TOP) for piece in weight_pieces]
    columns = columns + [tile_part[:, entry].astype(jnp.float32) for entry in range(TOP)]
    columns = columns + [tile_slot[:, entry].astype(jnp.float32) for entry in range(TOP)]
    extra = jnp.stack(columns, axis=1).astype(jnp.bfloat16)
    extra = jnp.broadcast_to(extra[None], (mem_local,) + extra.shape)
    flow = jnp.stack(three_pieces(initial_flow.T), axis=2).astype(jnp.bfloat16)
    flow = jnp.pad(flow, ((0, 0), (0, tile_local - basin_local), (0, width - hour_feat - 5 * TOP - 3)))
    send = jnp.concatenate([jnp.swapaxes(forcing, 0, 1), extra, flow], axis=2)
    send = jnp.broadcast_to(send[:, None], (mem_local, groups, tile_local, width))
    send = send.reshape(part_count, tile_local, width)
    arrived = lax.all_to_all(send, "basin", split_axis=0, concat_axis=0, tiled=True)

    vmem = pl.BlockSpec(memory_space=pltpu.VMEM)
    sources = min(part_count, 8)
    lateral = pl.pallas_call(
        functools.partial(lstm_kernel, (hour_feat, basin_local, groups, sources)),
        out_shape=jax.ShapeDtypeStruct((8, rows), jnp.float32),
        in_specs=[vmem] * 7,
        out_specs=vmem,
        compiler_params=pltpu.CompilerParams(vmem_limit_bytes=48 << 20),
    )(
        arrived,
        w_input,
        w_encoder,
        b_encoder[None],
        w_decoder,
        b_decoder[None],
        jnp.broadcast_to(w_output[None], (8, w_output.shape[0])),
    )
    axes = ("member", "basin")
    world = lax.axis_size("member") * part_count
    copies = jnp.broadcast_to(lateral[None], (world,) + lateral.shape)
    gathered = lax.all_to_all(copies, axes, split_axis=0, concat_axis=0, tiled=True)
    if reaches > KERNEL_REACHES or rows != LANES:
        return route_plain(gathered, upstream, reach_level, celerity, storage, mem_local, basin_local)
    discharge, ensemble = pl.pallas_call(
        functools.partial(route_kernel, mem_local, basin_local),
        out_shape=(
            jax.ShapeDtypeStruct((DEC, mem_local, basin_local), jnp.float32),
            jax.ShapeDtypeStruct((DEC, basin_local), jnp.float32),
        ),
        in_specs=[vmem] * 5,
        out_specs=(vmem, vmem),
        compiler_params=pltpu.CompilerParams(vmem_limit_bytes=48 << 20),
    )(
        gathered.reshape(world * 8, rows),
        upstream.T,
        reach_level[None],

        celerity[None],
        storage[None],
    )
    return jnp.transpose(discharge, (2, 1, 0)), ensemble.T


def solution(mesh):
    placed = (
        P("basin", "member", None),
        P("basin", None),
        P("basin", None),
        P("basin", None),
        P(),
        P(),
        P(),
        P(),
        P(),
        P(),
        P(),
        P(),
        P("basin", "member"),
        P(),
        P(),
    )
    return jax.shard_map(
        on_device,
        mesh=mesh,
        in_specs=placed,
        out_specs=(P("basin", "member", None), P("basin", None)),
        check_vma=False,
    )
```

```python
import functools

import jax
import jax.numpy as jnp
from jax import lax
from jax.experimental import pallas as pl
from jax.experimental.pallas import tpu as pltpu
from jax.sharding import PartitionSpec as P

FEAT = 8
DEC = 6
TOP = 2
LEVELS = 4
NEWTON = 4
BETA = 0.6
LANES = 128
KERNEL_REACHES = 512
EXTRAS = 16

dot = functools.partial(jnp.dot, preferred_element_type=jnp.float32)


def cell_update(gate_sum, memory_cell):
    units = memory_cell.shape[-1]
    input_gate = 0.5 * jnp.tanh(0.5 * gate_sum[:, :units]) + 0.5
    forget_gate = 0.5 * jnp.tanh(0.5 * gate_sum[:, units : 2 * units]) + 0.5
    candidate = jnp.tanh(gate_sum[:, 2 * units : 3 * units])
    output_gate = 0.5 * jnp.tanh(0.5 * gate_sum[:, 3 * units :]) + 0.5
    memory_cell = forget_gate * memory_cell + input_gate * candidate
    hidden = (output_gate * jnp.tanh(memory_cell)).astype(jnp.bfloat16)
    return hidden, memory_cell


def pack_kernel(
    forcing, part, slot, weight, flow, b_encoder, b_decoder, tables, send, small
):
    members, tile_local, width = forcing.shape
    groups = send.shape[0] // members
    basin_local = flow.shape[1]
    half = tile_local // 2

    def pieces(values):
        high = values.astype(jnp.bfloat16).astype(jnp.float32)
        rest = values - high
        middle = rest.astype(jnp.bfloat16).astype(jnp.float32)
        return [high, middle, rest - middle]

    def side_by_side(rows):
        return jnp.concatenate([rows[entry : entry + 1] for entry in range(TOP)], axis=1)

    common = pieces(side_by_side(weight[...]))
    common += [side_by_side(part[...].astype(jnp.float32)), side_by_side(slot[...].astype(jnp.float32))]
    owners = LANES // basin_local
    lane = lax.broadcasted_iota(jnp.int32, (1, LANES), 1)
    mine = lane // basin_local == lax.rem(lax.axis_index("basin"), owners)
    for member in range(members):
        tiles = forcing[member]
        first = tiles[:, :LANES]
        second = jnp.concatenate([tiles[:half, LANES:], tiles[half:, LANES:]], axis=1)
        own_flow = jnp.concatenate([flow[member : member + 1, :]] * owners, axis=1)
        rows = common + pieces(jnp.where(mine, own_flow, 0.0))
        rows.append(jnp.zeros((EXTRAS - len(rows), LANES), jnp.float32))
        extras = jnp.concatenate(rows, axis=0).astype(jnp.bfloat16)
        for group in range(groups):
            device = member * groups + group
            send[device, :tile_local, :] = first
            send[device, tile_local : tile_local + half, :] = second
            send[device, tile_local + half :, :] = extras
    small[0:1, : b_encoder.shape[1]] = b_encoder[...]
    small[1:2, : b_decoder.shape[1]] = b_decoder[...]
    at = 2
    for table in tables:
        count, length = table.shape
        small[at : at + count, :length] = table[...].astype(jnp.float32)
        at += count


def lstm_kernel(
    shape, arrived, w_input, w_encoder, w_decoder, w_output, small, out
):
    hour_feat, tile_local, basin_local, groups, sources = shape
    hours = hour_feat // FEAT
    devices = arrived.shape[0]
    rows = out.shape[1]
    units = w_encoder.shape[0]
    half = lax.rem(lax.axis_index("basin"), groups)
    first = (half * rows).astype(jnp.float32)
    folded = tile_local // 2
    extra_at = tile_local + folded

    def add_sources(chunk, total):
        block = arrived[pl.ds(chunk * sources, sources)].astype(jnp.float32)
        extras = block[:, extra_at:, :]
        weight = extras[:, 0] + extras[:, 1] + extras[:, 2]
        basin = extras[:, 3] * basin_local + extras[:, 4] - first
        weight = weight.T
        row_of = lax.broadcasted_iota(jnp.int32, (rows, TOP * tile_local), 0).astype(jnp.float32)
        picked, terms = [], []
        for source in range(sources):
            picked.append(jnp.where(row_of == basin[source : source + 1], 1.0, 0.0).astype(jnp.bfloat16))
            second = block[source, tile_local:extra_at, :]
            second = jnp.concatenate([second, pltpu.roll(second, LANES // 2, 1)], axis=0)
            tiles = jnp.concatenate([block[source, :tile_local, :], second], axis=1)
            for entry in range(TOP):
                column = weight[entry * tile_local : (entry + 1) * tile_local, source : source + 1]
                terms.append((column * tiles).astype(jnp.bfloat16))
        return total + dot(jnp.concatenate(picked, axis=1), jnp.concatenate(terms, axis=0))

    total = jnp.zeros((rows, 2 * LANES), jnp.float32)
    if devices == sources:
        total = add_sources(0, total)
    else:
        total = lax.fori_loop(0, devices // sources, add_sources, total)
    inputs = total.astype(jnp.bfloat16)

    owners = rows // basin_local
    flow = arrived[pl.ds(half * owners, owners), extra_at:, :].astype(jnp.float32)
    flow = jnp.sum(flow, axis=0)
    out[DEC : DEC + 1, :] = flow[5:6] + flow[6:7] + flow[7:8]
    out[DEC + 1 :, :] = jnp.zeros((out.shape[0] - DEC - 1, rows), jnp.float32)
    b_encoder, b_decoder = small[0:1, : 4 * units], small[1:2, : 4 * units]

    hidden = jnp.zeros((rows, units), jnp.bfloat16)
    memory_cell = jnp.zeros((rows, units), jnp.float32)
    for hour in range(hours):
        gate_sum = dot(inputs[:, hour * FEAT : (hour + 1) * FEAT], w_input[...]) + b_encoder
        gate_sum = gate_sum + dot(hidden, w_encoder[...])
        hidden, memory_cell = cell_update(gate_sum, memory_cell)
    for hour in range(DEC):
        gate_sum = dot(hidden, w_decoder[...]) + b_decoder
        hidden, memory_cell = cell_update(gate_sum, memory_cell)
        runoff = lax.dot_general(
            w_output[...], hidden, (((1,), (1,)), ((), ())), preferred_element_type=jnp.float32
        )[0:1]
        runoff = jnp.maximum(runoff, 0.0) + jnp.log(1.0 + jnp.exp(-jnp.abs(runoff)))
        out[hour : hour + 1, :] = runoff


def power(flow):
    return jnp.exp(BETA * jnp.log(flow))


def route_kernel(member_local, basin_local, reaches, gathered, small, discharge, ensemble):
    celerity, storage, level_row = small[2:3, :reaches], small[3:4, :reaches], small[4:5, :reaches]
    upstream = small[5:9, :reaches]
    halves = reaches // LANES
    per_member = halves * 8
    members = gathered.shape[0] // per_member
    levels = jnp.broadcast_to(level_row, (members, reaches)).astype(jnp.int32)
    source = lax.broadcasted_iota(jnp.int32, (reaches, reaches), 0).astype(jnp.float32)
    links = jnp.zeros((reaches, reaches), jnp.float32)
    for entry in range(upstream.shape[0]):
        links = links + jnp.where(source == upstream[entry : entry + 1, :], 1.0, 0.0)
    links = links.astype(jnp.bfloat16)
    speed_rate = jnp.broadcast_to(celerity, (members, reaches))
    store_rate = jnp.broadcast_to(storage, (members, reaches))

    def row(k):
        return jnp.concatenate(
            [gathered[pl.ds(h * 8 + k, members, stride=per_member), :] for h in range(halves)], axis=1
        )

    lateral = [row(k) for k in range(DEC)]
    current = row(DEC)
    powered = power(current)
    series = [jnp.zeros((members, reaches), jnp.float32) for _ in range(DEC)]
    for step in range(DEC + LEVELS - 1):
        target = jnp.zeros((members, reaches), jnp.float32)
        parts, owners = [], []
        for level in range(LEVELS):
            hour = step - level
            if 0 <= hour < DEC:
                target = jnp.where(levels == level, lateral[hour], target)
                if level:
                    flow = series[hour]
                    for _ in range(3):
                        piece = flow.astype(jnp.bfloat16)
                        parts.append(piece)
                        flow = flow - piece.astype(jnp.float32)
                    owners.append(level)
        if parts:
            sums = dot(jnp.concatenate(parts, axis=0), links)
            for i, level in enumerate(owners):
                at = 3 * i * members
                inflow = sums[at : at + members] + sums[at + members : at + 2 * members]
                inflow = inflow + sums[at + 2 * members : at + 3 * members]
                target = jnp.where(levels == level, target + speed_rate * inflow, target)
        target = target + store_rate * powered
        flow, flow_power = current, powered
        for _ in range(NEWTON):
            ratio = (target - (1.0 - BETA) * store_rate * flow_power) / (
                speed_rate * flow + BETA * store_rate * flow_power
            )
            flow = flow * jnp.maximum(ratio, 0.5)
            flow_power = power(flow)
        active = (levels <= step) & (levels > step - DEC)
        current = jnp.where(active, flow, current)
        powered = jnp.where(active, flow_power, powered)
        for level in range(LEVELS):
            hour = step - level
            if 0 <= hour < DEC:
                series[hour] = jnp.where(levels == level, flow, series[hour])
    column = lax.axis_index("basin") * basin_local
    mine = lax.axis_index("member")
    block = column // LANES
    shift = lax.rem(LANES - lax.rem(column, LANES), LANES)
    for hour in range(DEC):
        value = series[hour]
        picked = value[:, 0:LANES]
        for h in range(1, halves):
            picked = jnp.where(block == h, value[:, h * LANES : (h + 1) * LANES], picked)
        picked = pltpu.roll(picked, shift, 1)
        kept = picked[0:member_local]
        for q in range(1, members // member_local):
            kept = jnp.where(mine == q, picked[q * member_local : (q + 1) * member_local], kept)
        discharge[hour] = kept[:, 0:basin_local]
        mean = jnp.sum(picked, axis=0, keepdims=True) / members
        ensemble[hour : hour + 1, :] = mean[:, 0:basin_local]


def route_plain(gathered, upstream, reach_level, celerity, storage, mem_local, basin_local):
    reaches = reach_level.shape[0]
    members = gathered.shape[0] * gathered.shape[2] // reaches
    whole = gathered.reshape(members, -1, gathered.shape[1], gathered.shape[2])
    whole = jnp.transpose(whole, (1, 3, 0, 2)).reshape(reaches, members, gathered.shape[1])
    lateral, initial = whole[:, :, :DEC], whole[:, :, DEC]
    speed_rate, store_rate = celerity[:, None], storage[:, None]
    up_index = jnp.where(upstream < 0, reaches, upstream)
    outflow = jnp.zeros_like(lateral)
    for level_now in range(LEVELS):
        padded = jnp.concatenate([outflow, jnp.zeros_like(outflow[:1])], axis=0)
        inflow = padded[up_index[:, 0]]
        for entry in range(1, up_index.shape[1]):
            inflow = inflow + padded[up_index[:, entry]]
        flow = initial
        hours = []
        for hour in range(DEC):
            flow_power = flow**BETA
            target = speed_rate * inflow[:, :, hour] + store_rate * flow_power + lateral[:, :, hour]
            for _ in range(NEWTON):
                flow_power = flow**BETA
                ratio = (target - (1.0 - BETA) * store_rate * flow_power) / (
                    speed_rate * flow + BETA * store_rate * flow_power
                )
                flow = flow * jnp.maximum(ratio, 0.5)
            hours.append(flow)
        routed = jnp.stack(hours, axis=2)
        outflow = jnp.where((reach_level == level_now)[:, None, None], routed, outflow)
    ensemble = jnp.sum(outflow, axis=1) / members
    first_row = lax.axis_index("basin") * basin_local
    mine = lax.dynamic_slice_in_dim(outflow, first_row, basin_local, 0)
    mine = lax.dynamic_slice_in_dim(mine, lax.axis_index("member") * mem_local, mem_local, 1)
    return mine, lax.dynamic_slice_in_dim(ensemble, first_row, basin_local, 0)


def on_device(
    forcing,
    tile_part,
    tile_slot,
    tile_weight,
    w_input,
    w_encoder,
    b_encoder,
    w_decoder,
    b_decoder,
    w_output,
    celerity,
    storage,
    initial_flow,
    reach_level,
    upstream,
):
    tile_local, mem_local, hour_feat = forcing.shape
    part_count = lax.axis_size("basin")
    basin_local = initial_flow.shape[0]
    reaches = reach_level.shape[0]
    groups = part_count // mem_local
    rows = reaches // groups
    in_kernel = reaches <= KERNEL_REACHES and rows == LANES
    tables = (celerity[None], storage[None], reach_level[None], upstream.T) if in_kernel else ()

    vmem = pl.BlockSpec(memory_space=pltpu.VMEM)
    params = pltpu.CompilerParams(vmem_limit_bytes=48 << 20)
    send, small = pl.pallas_call(
        pack_kernel,
        out_shape=(
            jax.ShapeDtypeStruct((part_count, tile_local + tile_local // 2 + EXTRAS, LANES), jnp.bfloat16),
            jax.ShapeDtypeStruct((16, b_encoder.shape[0]), jnp.float32),
        ),
        in_specs=[vmem] * 7 + [(vmem,) * len(tables)],
        out_specs=(vmem, vmem),
        compiler_params=params,
    )(
        jnp.swapaxes(forcing, 0, 1),
        tile_part.T,
        tile_slot.T,
        tile_weight.T,
        initial_flow.T,
        b_encoder[None],
        b_decoder[None],
        tables,
    )
    arrived = lax.all_to_all(send, "basin", split_axis=0, concat_axis=0, tiled=True)
    sources = min(part_count, 8)
    lateral = pl.pallas_call(
        functools.partial(lstm_kernel, (hour_feat, tile_local, basin_local, groups, sources)),
        out_shape=jax.ShapeDtypeStruct((8, rows), jnp.float32),
        in_specs=[vmem] * 6,
        out_specs=vmem,
        compiler_params=params,
    )(
        arrived,
        w_input,
        w_encoder,
        w_decoder,
        jnp.broadcast_to(w_output[None], (8, w_output.shape[0])),
        small,
    )
    axes = ("member", "basin")
    world = lax.axis_size("member") * part_count
    copies = jnp.broadcast_to(lateral[None], (world,) + lateral.shape)
    gathered = lax.all_to_all(copies, axes, split_axis=0, concat_axis=0, tiled=True)
    if not in_kernel:
        return route_plain(gathered, upstream, reach_level, celerity, storage, mem_local, basin_local)
    discharge, ensemble = pl.pallas_call(
        functools.partial(route_kernel, mem_local, basin_local, reaches),
        out_shape=(
            jax.ShapeDtypeStruct((DEC, mem_local, basin_local), jnp.float32),
            jax.ShapeDtypeStruct((DEC, basin_local), jnp.float32),
        ),
        in_specs=[vmem] * 2,
        out_specs=(vmem, vmem),
        compiler_params=params,
    )(gathered.reshape(world * 8, rows), small)
    return jnp.transpose(discharge, (2, 1, 0)), ensemble.T


def solution(mesh):
    placed = (
        P("basin", "member", None),
        P("basin", None),
        P("basin", None),
        P("basin", None),
        P(),
        P(),
        P(),
        P(),
        P(),
        P(),
        P(),
        P(),
        P("basin", "member"),
        P(),
        P(),
    )
    return jax.shard_map(
        on_device,
        mesh=mesh,
        in_specs=placed,
        out_specs=(P("basin", "member", None), P("basin", None)),
        check_vma=False,
    )
```

```python
import functools

import jax
import jax.numpy as jnp
from jax import lax
from jax.experimental import pallas as pl
from jax.experimental.pallas import tpu as pltpu
from jax.sharding import PartitionSpec as P

FEAT = 8
DEC = 6
TOP = 2
LEVELS = 4
NEWTON = 4
BETA = 0.6
LANES = 128
KERNEL_REACHES = 512
EXTRAS = 16
INPUT_ROW = 16

dot = functools.partial(jnp.dot, preferred_element_type=jnp.float32)


def cell_update(gate_sum, memory_cell):
    units = memory_cell.shape[-1]
    input_gate = 0.5 * jnp.tanh(gate_sum[:, :units]) + 0.5
    forget_gate = 0.5 * jnp.tanh(gate_sum[:, units : 2 * units]) + 0.5
    candidate = jnp.tanh(gate_sum[:, 2 * units : 3 * units])
    output_gate = 0.5 * jnp.tanh(gate_sum[:, 3 * units :]) + 0.5
    memory_cell = forget_gate * memory_cell + input_gate * candidate
    hidden = (output_gate * jnp.tanh(memory_cell)).astype(jnp.bfloat16)
    return hidden, memory_cell


def stacked(height, width, parts):
    total = jnp.zeros((height, width), jnp.float32)
    at = 0
    for rows in parts:
        count, length = rows.shape
        total = total + jnp.pad(
            rows.astype(jnp.float32), ((at, height - at - count), (0, width - length))
        )
        at += count
    return total


def pack_kernel(basin_local, *refs):
    count = len(refs) // 2 - 1
    sources, send, held, semaphores = refs[:count], refs[count], refs[count + 1 : -1], refs[-1]
    copies = [
        pltpu.make_async_copy(source, target, semaphores.at[i])
        for i, (source, target) in enumerate(zip(sources, held, strict=True))
    ]
    for copy in copies:
        copy.start()
    for copy in copies:
        copy.wait()
    forcing, weight, part, slot, flow = held
    tile_local, members, width = forcing.shape
    groups = send.shape[0] // members
    half = tile_local // 2

    def pieces(values):
        high = values.astype(jnp.bfloat16).astype(jnp.float32)
        rest = values - high
        middle = rest.astype(jnp.bfloat16).astype(jnp.float32)
        return [high, middle, rest - middle]

    def side_by_side(rows):
        return jnp.concatenate([rows[entry : entry + 1] for entry in range(TOP)], axis=1)

    common = pieces(side_by_side(weight[...]))
    common += [side_by_side(part[...].astype(jnp.float32)), side_by_side(slot[...].astype(jnp.float32))]
    owners = LANES // basin_local
    lane = lax.broadcasted_iota(jnp.int32, (1, LANES), 1)
    mine = lane // basin_local == lax.rem(lax.axis_index("basin"), owners)
    for member in range(members):
        tiles = forcing[:, member, :]
        first = tiles[:, :LANES]
        second = jnp.concatenate([tiles[:half, LANES:], tiles[half:, LANES:]], axis=1)
        own_flow = flow[member : member + 1, :]
        own_flow = jnp.concatenate([own_flow] * owners, axis=1)
        rows = common + pieces(jnp.where(mine, own_flow, 0.0))
        rows.append(jnp.zeros((EXTRAS - len(rows), LANES), jnp.float32))
        extras = jnp.concatenate(rows, axis=0).astype(jnp.bfloat16)
        for group in range(groups):
            device = member * groups + group
            send[device, :tile_local, :] = first
            send[device, tile_local : tile_local + half, :] = second
            send[device, tile_local + half :, :] = extras


def lstm_kernel(
    shape, arrived, small, w_encoder, w_decoder, out
):
    hour_feat, tile_local, basin_local, groups, sources = shape
    hours = hour_feat // FEAT
    devices = arrived.shape[0]
    rows = out.shape[1]
    units = w_encoder.shape[0]
    half = lax.rem(lax.axis_index("basin"), groups)
    first = (half * rows).astype(jnp.float32)
    folded = tile_local // 2
    extra_at = tile_local + folded

    def add_sources(chunk, total):
        block = arrived[pl.ds(chunk * sources, sources)].astype(jnp.float32)
        extras = block[:, extra_at:, :]
        weight = extras[:, 0] + extras[:, 1] + extras[:, 2]
        basin = extras[:, 3] * basin_local + extras[:, 4] - first
        weight = weight.T
        row_of = lax.broadcasted_iota(jnp.int32, (rows, TOP * tile_local), 0).astype(jnp.float32)
        picked, terms = [], []
        for source in range(sources):
            picked.append(jnp.where(row_of == basin[source : source + 1], 1.0, 0.0).astype(jnp.bfloat16))
            second = block[source, tile_local:extra_at, :]
            second = jnp.concatenate([second, pltpu.roll(second, LANES // 2, 1)], axis=0)
            tiles = jnp.concatenate([block[source, :tile_local, :], second], axis=1)
            for entry in range(TOP):
                column = weight[entry * tile_local : (entry + 1) * tile_local, source : source + 1]
                terms.append((column * tiles).astype(jnp.bfloat16))
        return total + dot(jnp.concatenate(picked, axis=1), jnp.concatenate(terms, axis=0))

    total = jnp.zeros((rows, 2 * LANES), jnp.float32)
    if devices == sources:
        total = add_sources(0, total)
    else:
        total = lax.fori_loop(0, devices // sources, add_sources, total)
    inputs = total.astype(jnp.bfloat16)

    owners = rows // basin_local
    flow = arrived[pl.ds(half * owners, owners), extra_at:, :].astype(jnp.float32)
    flow = jnp.sum(flow, axis=0)
    out[DEC : DEC + 1, :] = flow[5:6] + flow[6:7] + flow[7:8]
    out[DEC + 1 :, :] = jnp.zeros((out.shape[0] - DEC - 1, rows), jnp.float32)
    b_encoder, b_decoder = small[0:1, : 4 * units], small[1:2, : 4 * units]
    w_input = small[INPUT_ROW : INPUT_ROW + FEAT, : 4 * units].astype(jnp.bfloat16)
    w_output = jnp.broadcast_to(small[2:3, :units], (8, units)).astype(jnp.bfloat16)

    hidden = jnp.zeros((rows, units), jnp.bfloat16)
    memory_cell = jnp.zeros((rows, units), jnp.float32)
    for hour in range(hours):
        gate_sum = dot(inputs[:, hour * FEAT : (hour + 1) * FEAT], w_input) + b_encoder
        gate_sum = gate_sum + dot(hidden, w_encoder[...])
        hidden, memory_cell = cell_update(gate_sum, memory_cell)
    for hour in range(DEC):
        gate_sum = dot(hidden, w_decoder[...]) + b_decoder
        hidden, memory_cell = cell_update(gate_sum, memory_cell)
        runoff = lax.dot_general(
            w_output, hidden, (((1,), (1,)), ((), ())), preferred_element_type=jnp.float32
        )[0:1]
        runoff = jnp.maximum(runoff, 0.0) + jnp.log(1.0 + jnp.exp(-jnp.abs(runoff)))
        out[hour : hour + 1, :] = runoff


def power(flow):
    return jnp.exp(BETA * jnp.log(flow))


def route_kernel(member_local, basin_local, reaches, gathered, small, discharge, ensemble):
    celerity, storage, level_row = small[3:4, :reaches], small[4:5, :reaches], small[5:6, :reaches]
    upstream = small[6:10, :reaches]
    halves = reaches // LANES
    per_member = halves * 8
    members = gathered.shape[0] // per_member
    levels = jnp.broadcast_to(level_row, (members, reaches)).astype(jnp.int32)
    source = lax.broadcasted_iota(jnp.int32, (reaches, reaches), 0).astype(jnp.float32)
    links = jnp.zeros((reaches, reaches), jnp.float32)
    for entry in range(upstream.shape[0]):
        links = links + jnp.where(source == upstream[entry : entry + 1, :], 1.0, 0.0)
    links = links.astype(jnp.bfloat16)
    speed_rate = jnp.broadcast_to(celerity, (members, reaches))
    store_rate = jnp.broadcast_to(storage, (members, reaches))

    def row(k):
        return jnp.concatenate(
            [gathered[pl.ds(h * 8 + k, members, stride=per_member), :] for h in range(halves)], axis=1
        )

    lateral = [row(k) for k in range(DEC)]
    current = row(DEC)
    powered = power(current)
    series = [jnp.zeros((members, reaches), jnp.float32) for _ in range(DEC)]
    for step in range(DEC + LEVELS - 1):
        target = jnp.zeros((members, reaches), jnp.float32)
        parts, owners = [], []
        for level in range(LEVELS):
            hour = step - level
            if 0 <= hour < DEC:
                target = jnp.where(levels == level, lateral[hour], target)
                if level:
                    flow = series[hour]
                    for _ in range(3):
                        piece = flow.astype(jnp.bfloat16)
                        parts.append(piece)
                        flow = flow - piece.astype(jnp.float32)
                    owners.append(level)
        if parts:
            sums = dot(jnp.concatenate(parts, axis=0), links)
            for i, level in enumerate(owners):
                at = 3 * i * members
                inflow = sums[at : at + members] + sums[at + members : at + 2 * members]
                inflow = inflow + sums[at + 2 * members : at + 3 * members]
                target = jnp.where(levels == level, target + speed_rate * inflow, target)
        target = target + store_rate * powered
        flow, flow_power = current, powered
        for _ in range(NEWTON):
            ratio = (target - (1.0 - BETA) * store_rate * flow_power) / (
                speed_rate * flow + BETA * store_rate * flow_power
            )
            flow = flow * jnp.maximum(ratio, 0.5)
            flow_power = power(flow)
        active = (levels <= step) & (levels > step - DEC)
        current = jnp.where(active, flow, current)
        powered = jnp.where(active, flow_power, powered)
        for level in range(LEVELS):
            hour = step - level
            if 0 <= hour < DEC:
                series[hour] = jnp.where(levels == level, flow, series[hour])
    column = lax.axis_index("basin") * basin_local
    mine = lax.axis_index("member")
    block = column // LANES
    shift = lax.rem(LANES - lax.rem(column, LANES), LANES)
    for hour in range(DEC):
        value = series[hour]
        picked = value[:, 0:LANES]
        for h in range(1, halves):
            picked = jnp.where(block == h, value[:, h * LANES : (h + 1) * LANES], picked)
        picked = pltpu.roll(picked, shift, 1)
        kept = picked[0:member_local]
        for q in range(1, members // member_local):
            kept = jnp.where(mine == q, picked[q * member_local : (q + 1) * member_local], kept)
        discharge[hour] = kept[:, 0:basin_local]
        mean = jnp.sum(picked, axis=0, keepdims=True) / members
        ensemble[hour : hour + 1, :] = mean[:, 0:basin_local]


def route_plain(gathered, upstream, reach_level, celerity, storage, mem_local, basin_local):
    reaches = reach_level.shape[0]
    members = gathered.shape[0] * gathered.shape[2] // reaches
    whole = gathered.reshape(members, -1, gathered.shape[1], gathered.shape[2])
    whole = jnp.transpose(whole, (1, 3, 0, 2)).reshape(reaches, members, gathered.shape[1])
    lateral, initial = whole[:, :, :DEC], whole[:, :, DEC]
    speed_rate, store_rate = celerity[:, None], storage[:, None]
    up_index = jnp.where(upstream < 0, reaches, upstream)
    outflow = jnp.zeros_like(lateral)
    for level_now in range(LEVELS):
        padded = jnp.concatenate([outflow, jnp.zeros_like(outflow[:1])], axis=0)
        inflow = padded[up_index[:, 0]]
        for entry in range(1, up_index.shape[1]):
            inflow = inflow + padded[up_index[:, entry]]
        flow = initial
        hours = []
        for hour in range(DEC):
            flow_power = flow**BETA
            target = speed_rate * inflow[:, :, hour] + store_rate * flow_power + lateral[:, :, hour]
            for _ in range(NEWTON):
                flow_power = flow**BETA
                ratio = (target - (1.0 - BETA) * store_rate * flow_power) / (
                    speed_rate * flow + BETA * store_rate * flow_power
                )
                flow = flow * jnp.maximum(ratio, 0.5)
            hours.append(flow)
        routed = jnp.stack(hours, axis=2)
        outflow = jnp.where((reach_level == level_now)[:, None, None], routed, outflow)
    ensemble = jnp.sum(outflow, axis=1) / members
    first_row = lax.axis_index("basin") * basin_local
    mine = lax.dynamic_slice_in_dim(outflow, first_row, basin_local, 0)
    mine = lax.dynamic_slice_in_dim(mine, lax.axis_index("member") * mem_local, mem_local, 1)
    return mine, lax.dynamic_slice_in_dim(ensemble, first_row, basin_local, 0)


def on_device(
    forcing,
    tile_part,
    tile_slot,
    tile_weight,
    w_input,
    w_encoder,
    b_encoder,
    w_decoder,
    b_decoder,
    w_output,
    celerity,
    storage,
    initial_flow,
    reach_level,
    upstream,
):
    tile_local, mem_local, hour_feat = forcing.shape
    part_count = lax.axis_size("basin")
    basin_local = initial_flow.shape[0]
    reaches = reach_level.shape[0]
    groups = part_count // mem_local
    rows = reaches // groups
    in_kernel = reaches <= KERNEL_REACHES and rows == LANES
    tables = (celerity[None], storage[None], reach_level[None], upstream.T) if in_kernel else ()

    vmem = pl.BlockSpec(memory_space=pltpu.VMEM)
    params = pltpu.CompilerParams(vmem_limit_bytes=48 << 20)
    operands = (forcing, tile_weight.T, tile_part.T, tile_slot.T, initial_flow.T)
    send = pl.pallas_call(
        functools.partial(pack_kernel, basin_local),
        out_shape=jax.ShapeDtypeStruct(
            (part_count, tile_local + tile_local // 2 + EXTRAS, LANES), jnp.bfloat16
        ),
        in_specs=[pl.BlockSpec(memory_space=pltpu.HBM)] * len(operands),
        out_specs=vmem,
        scratch_shapes=[pltpu.VMEM(x.shape, x.dtype) for x in operands]
        + [pltpu.SemaphoreType.DMA((len(operands),))],
        compiler_params=pltpu.CompilerParams(vmem_limit_bytes=60 << 20),
    )(*operands)
    arrived = lax.all_to_all(send, "basin", split_axis=0, concat_axis=0, tiled=True)
    sources = min(part_count, 8)
    units = w_encoder.shape[0]
    scale = jnp.where(jnp.arange(4 * units) // units == 2, 1.0, 0.5).astype(jnp.float32)
    shared = (b_encoder[None] * scale, b_decoder[None] * scale, w_output[None], *tables)
    blank = jnp.zeros((INPUT_ROW - sum(x.shape[0] for x in shared), 1), jnp.float32)
    small = stacked(INPUT_ROW + FEAT, 4 * units, (*shared, blank, w_input * scale))
    w_encoder = (w_encoder * scale).astype(jnp.bfloat16)
    w_decoder = (w_decoder * scale).astype(jnp.bfloat16)
    lateral = pl.pallas_call(
        functools.partial(lstm_kernel, (hour_feat, tile_local, basin_local, groups, sources)),
        out_shape=jax.ShapeDtypeStruct((8, rows), jnp.float32),
        in_specs=[vmem] * 4,
        out_specs=vmem,
        compiler_params=params,
    )(arrived, small, w_encoder, w_decoder)
    axes = ("member", "basin")
    world = lax.axis_size("member") * part_count
    copies = jnp.broadcast_to(lateral[None], (world,) + lateral.shape)
    gathered = lax.all_to_all(copies, axes, split_axis=0, concat_axis=0, tiled=True)
    if not in_kernel:
        return route_plain(gathered, upstream, reach_level, celerity, storage, mem_local, basin_local)
    discharge, ensemble = pl.pallas_call(
        functools.partial(route_kernel, mem_local, basin_local, reaches),
        out_shape=(
            jax.ShapeDtypeStruct((DEC, mem_local, basin_local), jnp.float32),
            jax.ShapeDtypeStruct((DEC, basin_local), jnp.float32),
        ),
        in_specs=[vmem] * 2,
        out_specs=(vmem, vmem),
        compiler_params=params,
    )(gathered.reshape(world * 8, rows), small)
    return jnp.transpose(discharge, (2, 1, 0)), ensemble.T


def solution(mesh):
    placed = (
        P("basin", "member", None),
        P("basin", None),
        P("basin", None),
        P("basin", None),
        P(),
        P(),
        P(),
        P(),
        P(),
        P(),
        P(),
        P(),
        P("basin", "member"),
        P(),
        P(),
    )
    return jax.shard_map(
        on_device,
        mesh=mesh,
        in_specs=placed,
        out_specs=(P("basin", "member", None), P("basin", None)),
        check_vma=False,
    )
```

```python
import functools

import jax
import jax.numpy as jnp
from jax import lax
from jax.experimental import pallas as pl
from jax.experimental.pallas import tpu as pltpu
from jax.sharding import PartitionSpec as P

FEAT = 8
DEC = 6
TOP = 2
LEVELS = 4
NEWTON = 4
BETA = 0.6
LANES = 128
KERNEL_REACHES = 512
EXTRAS = 16
INPUT_ROW = 16

dot = functools.partial(jnp.dot, preferred_element_type=jnp.float32)


def cell_update(gate_sum, memory_cell):
    units = memory_cell.shape[-1]
    input_gate = 0.5 * jnp.tanh(gate_sum[:, :units]) + 0.5
    candidate = jnp.tanh(gate_sum[:, 2 * units : 3 * units])
    kept = 0.5 * memory_cell
    fresh = kept + input_gate * candidate
    memory_cell = jnp.tanh(gate_sum[:, units : 2 * units]) * kept + fresh
    output_gate = 0.5 * jnp.tanh(gate_sum[:, 3 * units :]) + 0.5
    hidden = (output_gate * jnp.tanh(memory_cell)).astype(jnp.bfloat16)
    return hidden, memory_cell


def stacked(height, width, parts):
    total = jnp.zeros((height, width), jnp.float32)
    at = 0
    for rows in parts:
        count, length = rows.shape
        total = total + jnp.pad(
            rows.astype(jnp.float32), ((at, height - at - count), (0, width - length))
        )
        at += count
    return total


def pack_kernel(basin_local, *refs):
    count = len(refs) // 2 - 1
    sources, send, held, semaphores = refs[:count], refs[count], refs[count + 1 : -1], refs[-1]
    copies = [
        pltpu.make_async_copy(source, target, semaphores.at[i])
        for i, (source, target) in enumerate(zip(sources, held, strict=True))
    ]
    for copy in copies:
        copy.start()
    for copy in copies:
        copy.wait()
    forcing, weight, part, slot, flow = held
    tile_local, members, width = forcing.shape
    groups = send.shape[0] // members
    half = tile_local // 2

    def pieces(values):
        high = values.astype(jnp.bfloat16).astype(jnp.float32)
        rest = values - high
        middle = rest.astype(jnp.bfloat16).astype(jnp.float32)
        return [high, middle, rest - middle]

    def side_by_side(rows):
        return jnp.concatenate([rows[entry : entry + 1] for entry in range(TOP)], axis=1)

    common = pieces(side_by_side(weight[...]))
    common += [side_by_side(part[...].astype(jnp.float32)), side_by_side(slot[...].astype(jnp.float32))]
    owners = LANES // basin_local
    lane = lax.broadcasted_iota(jnp.int32, (1, LANES), 1)
    mine = lane // basin_local == lax.rem(lax.axis_index("basin"), owners)
    for member in range(members):
        tiles = forcing[:, member, :]
        first = tiles[:, :LANES]
        second = jnp.concatenate([tiles[:half, LANES:], tiles[half:, LANES:]], axis=1)
        own_flow = flow[member : member + 1, :]
        own_flow = jnp.concatenate([own_flow] * owners, axis=1)
        rows = common + pieces(jnp.where(mine, own_flow, 0.0))
        rows.append(jnp.zeros((EXTRAS - len(rows), LANES), jnp.float32))
        extras = jnp.concatenate(rows, axis=0).astype(jnp.bfloat16)
        for group in range(groups):
            device = member * groups + group
            send[device, :tile_local, :] = first
            send[device, tile_local : tile_local + half, :] = second
            send[device, tile_local + half :, :] = extras


def lstm_kernel(
    shape, arrived, small, w_encoder, w_decoder, out
):
    hour_feat, tile_local, basin_local, groups, sources = shape
    hours = hour_feat // FEAT
    devices = arrived.shape[0]
    rows = out.shape[1]
    units = w_encoder.shape[0]
    half = lax.rem(lax.axis_index("basin"), groups)
    first = (half * rows).astype(jnp.float32)
    folded = tile_local // 2
    extra_at = tile_local + folded

    def add_sources(chunk, total):
        block = arrived[pl.ds(chunk * sources, sources)].astype(jnp.float32)
        extras = block[:, extra_at:, :]
        weight = extras[:, 0] + extras[:, 1] + extras[:, 2]
        basin = extras[:, 3] * basin_local + extras[:, 4] - first
        weight = weight.T
        row_of = lax.broadcasted_iota(jnp.int32, (rows, TOP * tile_local), 0).astype(jnp.float32)
        picked, terms = [], []
        for source in range(sources):
            picked.append(jnp.where(row_of == basin[source : source + 1], 1.0, 0.0).astype(jnp.bfloat16))
            second = block[source, tile_local:extra_at, :]
            second = jnp.concatenate([second, pltpu.roll(second, LANES // 2, 1)], axis=0)
            tiles = jnp.concatenate([block[source, :tile_local, :], second], axis=1)
            for entry in range(TOP):
                column = weight[entry * tile_local : (entry + 1) * tile_local, source : source + 1]
                terms.append((column * tiles).astype(jnp.bfloat16))
        return total + dot(jnp.concatenate(picked, axis=1), jnp.concatenate(terms, axis=0))

    total = jnp.zeros((rows, 2 * LANES), jnp.float32)
    if devices == sources:
        total = add_sources(0, total)
    else:
        total = lax.fori_loop(0, devices // sources, add_sources, total)
    inputs = total.astype(jnp.bfloat16)

    owners = rows // basin_local
    flow = arrived[pl.ds(half * owners, owners), extra_at:, :].astype(jnp.float32)
    flow = jnp.sum(flow, axis=0)
    out[DEC : DEC + 1, :] = flow[5:6] + flow[6:7] + flow[7:8]
    out[DEC + 1 :, :] = jnp.zeros((out.shape[0] - DEC - 1, rows), jnp.float32)
    b_encoder, b_decoder = small[0:1, : 4 * units], small[1:2, : 4 * units]
    w_input = small[INPUT_ROW : INPUT_ROW + FEAT, : 4 * units].astype(jnp.bfloat16)
    w_output = jnp.broadcast_to(small[2:3, :units], (8, units)).astype(jnp.bfloat16)

    hidden = jnp.zeros((rows, units), jnp.bfloat16)
    memory_cell = jnp.zeros((rows, units), jnp.float32)
    ahead = dot(inputs[:, :FEAT], w_input) + b_encoder
    for hour in range(hours):
        gate_sum = ahead + dot(hidden, w_encoder[...]) if hour else ahead
        if hour + 1 < hours:
            ahead = dot(inputs[:, (hour + 1) * FEAT : (hour + 2) * FEAT], w_input) + b_encoder
        hidden, memory_cell = cell_update(gate_sum, memory_cell)
    for hour in range(DEC):
        gate_sum = dot(hidden, w_decoder[...]) + b_decoder
        hidden, memory_cell = cell_update(gate_sum, memory_cell)
        runoff = lax.dot_general(
            w_output, hidden, (((1,), (1,)), ((), ())), preferred_element_type=jnp.float32
        )[0:1]
        runoff = jnp.maximum(runoff, 0.0) + jnp.log(1.0 + jnp.exp(-jnp.abs(runoff)))
        out[hour : hour + 1, :] = runoff


def power(flow):
    return jnp.exp(BETA * jnp.log(flow))


def route_kernel(member_local, basin_local, reaches, gathered, small, discharge, ensemble):
    celerity, storage, level_row = small[3:4, :reaches], small[4:5, :reaches], small[5:6, :reaches]
    upstream = small[6:10, :reaches]
    halves = reaches // LANES
    per_member = halves * 8
    members = gathered.shape[0] // per_member
    shape = (members, LANES)

    def spread(row):
        return [jnp.broadcast_to(row[:, h * LANES : (h + 1) * LANES], shape) for h in range(halves)]

    def pick(parts, index):
        out = None
        for h, part in enumerate(parts):
            value = jnp.take_along_axis(part, index % LANES, axis=1)
            out = value if out is None else jnp.where(index // LANES == h, value, out)
        return out

    level_parts = spread(level_row.astype(jnp.int32))
    levels = jnp.concatenate(level_parts, axis=1)
    sources, lags = [], []
    for entry in range(upstream.shape[0]):
        named = spread(upstream[entry : entry + 1, :].astype(jnp.int32))
        index = [jnp.maximum(x, 0) for x in named]
        sources.append(index)
        lags.append(
            [jnp.where(x < 0, 0, level - pick(level_parts, i)) for x, level, i in zip(named, level_parts, index, strict=True)]
        )

    def handed_on(flow):
        parts = [flow[:, h * LANES : (h + 1) * LANES] for h in range(halves)]
        sums = [[jnp.zeros(shape, jnp.float32)] * halves for _ in range(LEVELS - 1)]
        for index, lag in zip(sources, lags, strict=True):
            for h in range(halves):
                value = pick(parts, index[h])
                for k in range(LEVELS - 1):
                    sums[k][h] = sums[k][h] + jnp.where(lag[h] == k + 1, value, 0.0)
        return [jnp.concatenate(x, axis=1) for x in sums]

    speed_rate = jnp.broadcast_to(celerity, (members, reaches))
    store_rate = jnp.broadcast_to(storage, (members, reaches))

    def row(k):
        return jnp.concatenate(
            [gathered[pl.ds(h * 8 + k, members, stride=per_member), :] for h in range(halves)], axis=1
        )

    lateral = [row(k) for k in range(DEC)]
    current = row(DEC)
    powered = power(current)
    series = [jnp.zeros((members, reaches), jnp.float32) for _ in range(DEC)]
    given = []
    for step in range(DEC + LEVELS - 1):
        target = store_rate * powered
        for level in range(LEVELS):
            hour = step - level
            if 0 <= hour < DEC:
                target = jnp.where(levels == level, target + lateral[hour], target)
        for k in range(LEVELS - 1):
            if step - 1 - k >= 0:
                target = target + speed_rate * given[step - 1 - k][k]
        flow, flow_power = current, powered
        for _ in range(NEWTON):
            ratio = (target - (1.0 - BETA) * store_rate * flow_power) / (
                speed_rate * flow + BETA * store_rate * flow_power
            )
            flow = flow * jnp.maximum(ratio, 0.5)
            flow_power = power(flow)
        active = (levels <= step) & (levels > step - DEC)
        current = jnp.where(active, flow, current)
        powered = jnp.where(active, flow_power, powered)
        given.append(handed_on(current) if step + 1 < DEC + LEVELS - 1 else None)
        for level in range(LEVELS):
            hour = step - level
            if 0 <= hour < DEC:
                series[hour] = jnp.where(levels == level, flow, series[hour])
    column = lax.axis_index("basin") * basin_local
    mine = lax.axis_index("member")
    block = column // LANES
    shift = lax.rem(LANES - lax.rem(column, LANES), LANES)
    for hour in range(DEC):
        value = series[hour]
        picked = value[:, 0:LANES]
        for h in range(1, halves):
            picked = jnp.where(block == h, value[:, h * LANES : (h + 1) * LANES], picked)
        picked = pltpu.roll(picked, shift, 1)
        kept = picked[0:member_local]
        for q in range(1, members // member_local):
            kept = jnp.where(mine == q, picked[q * member_local : (q + 1) * member_local], kept)
        discharge[hour] = kept[:, 0:basin_local]
        mean = jnp.sum(picked, axis=0, keepdims=True) / members
        ensemble[hour : hour + 1, :] = mean[:, 0:basin_local]


def route_plain(gathered, upstream, reach_level, celerity, storage, mem_local, basin_local):
    reaches = reach_level.shape[0]
    members = gathered.shape[0] * gathered.shape[2] // reaches
    whole = gathered.reshape(members, -1, gathered.shape[1], gathered.shape[2])
    whole = jnp.transpose(whole, (1, 3, 0, 2)).reshape(reaches, members, gathered.shape[1])
    lateral, initial = whole[:, :, :DEC], whole[:, :, DEC]
    speed_rate, store_rate = celerity[:, None], storage[:, None]
    up_index = jnp.where(upstream < 0, reaches, upstream)
    outflow = jnp.zeros_like(lateral)
    for level_now in range(LEVELS):
        padded = jnp.concatenate([outflow, jnp.zeros_like(outflow[:1])], axis=0)
        inflow = padded[up_index[:, 0]]
        for entry in range(1, up_index.shape[1]):
            inflow = inflow + padded[up_index[:, entry]]
        flow = initial
        hours = []
        for hour in range(DEC):
            flow_power = flow**BETA
            target = speed_rate * inflow[:, :, hour] + store_rate * flow_power + lateral[:, :, hour]
            for _ in range(NEWTON):
                flow_power = flow**BETA
                ratio = (target - (1.0 - BETA) * store_rate * flow_power) / (
                    speed_rate * flow + BETA * store_rate * flow_power
                )
                flow = flow * jnp.maximum(ratio, 0.5)
            hours.append(flow)
        routed = jnp.stack(hours, axis=2)
        outflow = jnp.where((reach_level == level_now)[:, None, None], routed, outflow)
    ensemble = jnp.sum(outflow, axis=1) / members
    first_row = lax.axis_index("basin") * basin_local
    mine = lax.dynamic_slice_in_dim(outflow, first_row, basin_local, 0)
    mine = lax.dynamic_slice_in_dim(mine, lax.axis_index("member") * mem_local, mem_local, 1)
    return mine, lax.dynamic_slice_in_dim(ensemble, first_row, basin_local, 0)


def on_device(
    forcing,
    tile_part,
    tile_slot,
    tile_weight,
    w_input,
    w_encoder,
    b_encoder,
    w_decoder,
    b_decoder,
    w_output,
    celerity,
    storage,
    initial_flow,
    reach_level,
    upstream,
):
    tile_local, mem_local, hour_feat = forcing.shape
    part_count = lax.axis_size("basin")
    basin_local = initial_flow.shape[0]
    reaches = reach_level.shape[0]
    groups = part_count // mem_local
    rows = reaches // groups
    in_kernel = reaches <= KERNEL_REACHES and rows == LANES
    tables = (celerity[None], storage[None], reach_level[None], upstream.T) if in_kernel else ()

    vmem = pl.BlockSpec(memory_space=pltpu.VMEM)
    params = pltpu.CompilerParams(vmem_limit_bytes=48 << 20)
    operands = (forcing, tile_weight.T, tile_part.T, tile_slot.T, initial_flow.T)
    send = pl.pallas_call(
        functools.partial(pack_kernel, basin_local),
        out_shape=jax.ShapeDtypeStruct(
            (part_count, tile_local + tile_local // 2 + EXTRAS, LANES), jnp.bfloat16
        ),
        in_specs=[pl.BlockSpec(memory_space=pltpu.HBM)] * len(operands),
        out_specs=vmem,
        scratch_shapes=[pltpu.VMEM(x.shape, x.dtype) for x in operands]
        + [pltpu.SemaphoreType.DMA((len(operands),))],
        compiler_params=pltpu.CompilerParams(vmem_limit_bytes=60 << 20),
    )(*operands)
    arrived = lax.all_to_all(send, "basin", split_axis=0, concat_axis=0, tiled=True)
    sources = min(part_count, 8)
    units = w_encoder.shape[0]
    scale = jnp.where(jnp.arange(4 * units) // units == 2, 1.0, 0.5).astype(jnp.float32)
    shared = (b_encoder[None] * scale, b_decoder[None] * scale, w_output[None], *tables)
    blank = jnp.zeros((INPUT_ROW - sum(x.shape[0] for x in shared), 1), jnp.float32)
    small = stacked(INPUT_ROW + FEAT, 4 * units, (*shared, blank, w_input * scale))
    w_encoder = (w_encoder * scale).astype(jnp.bfloat16)
    w_decoder = (w_decoder * scale).astype(jnp.bfloat16)
    lateral = pl.pallas_call(
        functools.partial(lstm_kernel, (hour_feat, tile_local, basin_local, groups, sources)),
        out_shape=jax.ShapeDtypeStruct((8, rows), jnp.float32),
        in_specs=[vmem] * 4,
        out_specs=vmem,
        compiler_params=params,
    )(arrived, small, w_encoder, w_decoder)
    axes = ("member", "basin")
    world = lax.axis_size("member") * part_count
    copies = jnp.broadcast_to(lateral[None], (world,) + lateral.shape)
    gathered = lax.all_to_all(copies, axes, split_axis=0, concat_axis=0, tiled=True)
    if not in_kernel:
        return route_plain(gathered, upstream, reach_level, celerity, storage, mem_local, basin_local)
    discharge, ensemble = pl.pallas_call(
        functools.partial(route_kernel, mem_local, basin_local, reaches),
        out_shape=(
            jax.ShapeDtypeStruct((DEC, mem_local, basin_local), jnp.float32),
            jax.ShapeDtypeStruct((DEC, basin_local), jnp.float32),
        ),
        in_specs=[vmem] * 2,
        out_specs=(vmem, vmem),
        compiler_params=params,
    )(gathered.reshape(world * 8, rows), small)
    return jnp.transpose(discharge, (2, 1, 0)), ensemble.T


def solution(mesh):
    placed = (
        P("basin", "member", None),
        P("basin", None),
        P("basin", None),
        P("basin", None),
        P(),
        P(),
        P(),
        P(),
        P(),
        P(),
        P(),
        P(),
        P("basin", "member"),
        P(),
        P(),
    )
    return jax.shard_map(
        on_device,
        mesh=mesh,
        in_specs=placed,
        out_specs=(P("basin", "member", None), P("basin", None)),
        check_vma=False,
    )
```

```python
import functools

import jax
import jax.numpy as jnp
from jax import lax
from jax.experimental import pallas as pl
from jax.experimental.pallas import tpu as pltpu
from jax.sharding import PartitionSpec as P

FEAT = 8
DEC = 6
TOP = 2
LEVELS = 4
NEWTON = 4
BETA = 0.6
LANES = 128
KERNEL_REACHES = 512
EXTRAS = 8
CARRIED = jnp.float16
HALF_STEP = 2.0**11
INPUT_ROW = 16

dot = functools.partial(jnp.dot, preferred_element_type=jnp.float32)


def cell_update(gate_sum, memory_cell):
    units = memory_cell.shape[-1]
    input_gate = 0.5 * jnp.tanh(gate_sum[:, :units]) + 0.5
    candidate = jnp.tanh(gate_sum[:, 2 * units : 3 * units])
    kept = 0.5 * memory_cell
    fresh = kept + input_gate * candidate
    memory_cell = jnp.tanh(gate_sum[:, units : 2 * units]) * kept + fresh
    output_gate = 0.5 * jnp.tanh(gate_sum[:, 3 * units :]) + 0.5
    hidden = (output_gate * jnp.tanh(memory_cell)).astype(jnp.bfloat16)
    return hidden, memory_cell


def stacked(height, width, parts):
    total = jnp.zeros((height, width), jnp.float32)
    at = 0
    for rows in parts:
        count, length = rows.shape
        total = total + jnp.pad(
            rows.astype(jnp.float32), ((at, height - at - count), (0, width - length))
        )
        at += count
    return total


def pack_kernel(basin_local, *refs):
    count = len(refs) // 2 - 1
    sources, send, held, semaphores = refs[:count], refs[count], refs[count + 1 : -1], refs[-1]
    copies = [
        pltpu.make_async_copy(source, target, semaphores.at[i])
        for i, (source, target) in enumerate(zip(sources, held, strict=True))
    ]
    for copy in copies:
        copy.start()
    for copy in copies:
        copy.wait()
    forcing, weight, part, slot, flow = held
    tile_local, members, width = forcing.shape
    groups = send.shape[0] // members
    half = tile_local // 2

    def pieces(values):
        high = values.astype(jnp.bfloat16).astype(jnp.float32)
        rest = values - high
        middle = rest.astype(jnp.bfloat16).astype(jnp.float32)
        return [high, middle, rest - middle]

    def side_by_side(rows):
        return jnp.concatenate([rows[entry : entry + 1] for entry in range(TOP)], axis=1)

    common = pieces(side_by_side(weight[...]))
    common += [side_by_side(part[...].astype(jnp.float32)), side_by_side(slot[...].astype(jnp.float32))]
    owners = LANES // basin_local
    lane = lax.broadcasted_iota(jnp.int32, (1, LANES), 1)
    mine = lane // basin_local == lax.rem(lax.axis_index("basin"), owners)
    for member in range(members):
        tiles = forcing[:, member, :]
        first = tiles[:, :LANES]
        second = jnp.concatenate([tiles[:half, LANES:], tiles[half:, LANES:]], axis=1)
        own_flow = flow[member : member + 1, :]
        own_flow = jnp.concatenate([own_flow] * owners, axis=1)
        rows = common + pieces(jnp.where(mine, own_flow, 0.0))
        extras = jnp.concatenate(rows, axis=0).astype(jnp.bfloat16)
        for group in range(groups):
            device = member * groups + group
            send[device, :tile_local, :] = first
            send[device, tile_local : tile_local + half, :] = second
            send[device, tile_local + half :, :] = extras


def encode(values):
    spread = values * (2.0**13 + 1.0)
    rounded = spread - (spread - values)
    place = (values - rounded) / jnp.maximum(rounded, 1e-30)
    digits = jnp.clip(jnp.floor(place * (1.5 * HALF_STEP) + 0.5), -1.0, 1.0)
    total = digits[0:1]
    for k in range(1, values.shape[0]):
        total = total + 3.0**k * digits[k : k + 1]
    return jnp.concatenate([rounded, total], axis=0)


def decode(rows):
    *rounded, total = rows
    values = []
    for row in rounded:
        above = jnp.floor(total * (1.0 / 3.0) + 0.5)
        values.append(row + row * ((total - 3.0 * above) * (1.0 / (1.5 * HALF_STEP))))
        total = above
    return values


def lstm_kernel(
    shape, arrived, small, w_encoder, w_decoder, out
):
    hour_feat, tile_local, basin_local, groups, sources = shape
    hours = hour_feat // FEAT
    devices = arrived.shape[0]
    rows = out.shape[1]
    units = w_encoder.shape[0]
    half = lax.rem(lax.axis_index("basin"), groups)
    first = (half * rows).astype(jnp.float32)
    folded = tile_local // 2
    extra_at = tile_local + folded

    def add_sources(chunk, total):
        block = arrived[pl.ds(chunk * sources, sources)].astype(jnp.float32)
        extras = block[:, extra_at:, :]
        weight = extras[:, 0] + extras[:, 1] + extras[:, 2]
        basin = extras[:, 3] * basin_local + extras[:, 4] - first
        weight = weight.T
        row_of = lax.broadcasted_iota(jnp.int32, (rows, TOP * tile_local), 0).astype(jnp.float32)
        picked, terms = [], []
        for source in range(sources):
            picked.append(jnp.where(row_of == basin[source : source + 1], 1.0, 0.0).astype(jnp.bfloat16))
            second = block[source, tile_local:extra_at, :]
            second = jnp.concatenate([second, pltpu.roll(second, LANES // 2, 1)], axis=0)
            tiles = jnp.concatenate([block[source, :tile_local, :], second], axis=1)
            for entry in range(TOP):
                column = weight[entry * tile_local : (entry + 1) * tile_local, source : source + 1]
                terms.append((column * tiles).astype(jnp.bfloat16))
        return total + dot(jnp.concatenate(picked, axis=1), jnp.concatenate(terms, axis=0))

    total = jnp.zeros((rows, 2 * LANES), jnp.float32)
    if devices == sources:
        total = add_sources(0, total)
    else:
        total = lax.fori_loop(0, devices // sources, add_sources, total)
    inputs = total.astype(jnp.bfloat16)

    owners = rows // basin_local
    flow = arrived[pl.ds(half * owners, owners), extra_at:, :].astype(jnp.float32)
    flow = jnp.sum(flow, axis=0)
    results = []
    b_encoder, b_decoder = small[0:1, : 4 * units], small[1:2, : 4 * units]
    w_input = small[INPUT_ROW : INPUT_ROW + FEAT, : 4 * units].astype(jnp.bfloat16)
    w_output = jnp.broadcast_to(small[2:3, :units], (8, units)).astype(jnp.bfloat16)

    hidden = jnp.zeros((rows, units), jnp.bfloat16)
    memory_cell = jnp.zeros((rows, units), jnp.float32)
    ahead = dot(inputs[:, :FEAT], w_input) + b_encoder
    for hour in range(hours):
        gate_sum = ahead + dot(hidden, w_encoder[...]) if hour else ahead
        if hour + 1 < hours:
            ahead = dot(inputs[:, (hour + 1) * FEAT : (hour + 2) * FEAT], w_input) + b_encoder
        hidden, memory_cell = cell_update(gate_sum, memory_cell)
    for hour in range(DEC):
        gate_sum = dot(hidden, w_decoder[...]) + b_decoder
        hidden, memory_cell = cell_update(gate_sum, memory_cell)
        runoff = lax.dot_general(
            w_output, hidden, (((1,), (1,)), ((), ())), preferred_element_type=jnp.float32
        )[0:1]
        runoff = jnp.maximum(runoff, 0.0) + jnp.log(1.0 + jnp.exp(-jnp.abs(runoff)))
        results.append(runoff)
    results.append(flow[5:6] + flow[6:7] + flow[7:8])
    out[...] = encode(jnp.concatenate(results, axis=0))


def power(flow):
    return jnp.exp(BETA * jnp.log(flow))


def route_kernel(member_local, basin_local, reaches, gathered, small, discharge, ensemble):
    celerity, storage, level_row = small[3:4, :reaches], small[4:5, :reaches], small[5:6, :reaches]
    upstream = small[6:10, :reaches]
    halves = reaches // LANES
    per_member = halves * 8
    members = gathered.shape[0] // per_member
    shape = (members, LANES)

    def spread(row):
        return [jnp.broadcast_to(row[:, h * LANES : (h + 1) * LANES], shape) for h in range(halves)]

    def pick(parts, index):
        out = None
        for h, part in enumerate(parts):
            value = jnp.take_along_axis(part, index % LANES, axis=1)
            out = value if out is None else jnp.where(index // LANES == h, value, out)
        return out

    level_parts = spread(level_row.astype(jnp.int32))
    levels = jnp.concatenate(level_parts, axis=1)
    sources, lags = [], []
    for entry in range(upstream.shape[0]):
        named = spread(upstream[entry : entry + 1, :].astype(jnp.int32))
        index = [jnp.maximum(x, 0) for x in named]
        sources.append(index)
        lags.append(
            [jnp.where(x < 0, 0, level - pick(level_parts, i)) for x, level, i in zip(named, level_parts, index, strict=True)]
        )

    def handed_on(flow):
        parts = [flow[:, h * LANES : (h + 1) * LANES] for h in range(halves)]
        sums = [[jnp.zeros(shape, jnp.float32)] * halves for _ in range(LEVELS - 1)]
        for index, lag in zip(sources, lags, strict=True):
            for h in range(halves):
                value = pick(parts, index[h])
                for k in range(LEVELS - 1):
                    sums[k][h] = sums[k][h] + jnp.where(lag[h] == k + 1, value, 0.0)
        return [jnp.concatenate(x, axis=1) for x in sums]

    speed_rate = jnp.broadcast_to(celerity, (members, reaches))
    store_rate = jnp.broadcast_to(storage, (members, reaches))

    def row(k):
        return jnp.concatenate(
            [gathered[pl.ds(h * 8 + k, members, stride=per_member), :] for h in range(halves)], axis=1
        )

    *lateral, current = decode([row(k) for k in range(8)])
    powered = power(current)
    series = [jnp.zeros((members, reaches), jnp.float32) for _ in range(DEC)]
    given = []
    for step in range(DEC + LEVELS - 1):
        target = store_rate * powered
        for level in range(LEVELS):
            hour = step - level
            if 0 <= hour < DEC:
                target = jnp.where(levels == level, target + lateral[hour], target)
        for k in range(LEVELS - 1):
            if step - 1 - k >= 0:
                target = target + speed_rate * given[step - 1 - k][k]
        flow, flow_power = current, powered
        for _ in range(NEWTON):
            ratio = (target - (1.0 - BETA) * store_rate * flow_power) / (
                speed_rate * flow + BETA * store_rate * flow_power
            )
            flow = flow * jnp.maximum(ratio, 0.5)
            flow_power = power(flow)
        active = (levels <= step) & (levels > step - DEC)
        current = jnp.where(active, flow, current)
        powered = jnp.where(active, flow_power, powered)
        given.append(handed_on(current) if step + 1 < DEC + LEVELS - 1 else None)
        for level in range(LEVELS):
            hour = step - level
            if 0 <= hour < DEC:
                series[hour] = jnp.where(levels == level, flow, series[hour])
    column = lax.axis_index("basin") * basin_local
    mine = lax.axis_index("member")
    block = column // LANES
    shift = lax.rem(LANES - lax.rem(column, LANES), LANES)
    for hour in range(DEC):
        value = series[hour]
        picked = value[:, 0:LANES]
        for h in range(1, halves):
            picked = jnp.where(block == h, value[:, h * LANES : (h + 1) * LANES], picked)
        picked = pltpu.roll(picked, shift, 1)
        kept = picked[0:member_local]
        for q in range(1, members // member_local):
            kept = jnp.where(mine == q, picked[q * member_local : (q + 1) * member_local], kept)
        discharge[hour] = kept[:, 0:basin_local]
        mean = jnp.sum(picked, axis=0, keepdims=True) / members
        ensemble[hour : hour + 1, :] = mean[:, 0:basin_local]


def route_plain(gathered, upstream, reach_level, celerity, storage, mem_local, basin_local):
    reaches = reach_level.shape[0]
    members = gathered.shape[0] * gathered.shape[2] // reaches
    whole = gathered.reshape(members, -1, gathered.shape[1], gathered.shape[2])
    whole = jnp.transpose(whole, (1, 3, 0, 2)).reshape(reaches, members, gathered.shape[1])
    *lateral, initial = decode([whole[:, :, k] for k in range(8)])
    lateral = jnp.stack(lateral, axis=2)
    speed_rate, store_rate = celerity[:, None], storage[:, None]
    up_index = jnp.where(upstream < 0, reaches, upstream)
    outflow = jnp.zeros_like(lateral)
    for level_now in range(LEVELS):
        padded = jnp.concatenate([outflow, jnp.zeros_like(outflow[:1])], axis=0)
        inflow = padded[up_index[:, 0]]
        for entry in range(1, up_index.shape[1]):
            inflow = inflow + padded[up_index[:, entry]]
        flow = initial
        hours = []
        for hour in range(DEC):
            flow_power = flow**BETA
            target = speed_rate * inflow[:, :, hour] + store_rate * flow_power + lateral[:, :, hour]
            for _ in range(NEWTON):
                flow_power = flow**BETA
                ratio = (target - (1.0 - BETA) * store_rate * flow_power) / (
                    speed_rate * flow + BETA * store_rate * flow_power
                )
                flow = flow * jnp.maximum(ratio, 0.5)
            hours.append(flow)
        routed = jnp.stack(hours, axis=2)
        outflow = jnp.where((reach_level == level_now)[:, None, None], routed, outflow)
    ensemble = jnp.sum(outflow, axis=1) / members
    first_row = lax.axis_index("basin") * basin_local
    mine = lax.dynamic_slice_in_dim(outflow, first_row, basin_local, 0)
    mine = lax.dynamic_slice_in_dim(mine, lax.axis_index("member") * mem_local, mem_local, 1)
    return mine, lax.dynamic_slice_in_dim(ensemble, first_row, basin_local, 0)


def on_device(
    forcing,
    tile_part,
    tile_slot,
    tile_weight,
    w_input,
    w_encoder,
    b_encoder,
    w_decoder,
    b_decoder,
    w_output,
    celerity,
    storage,
    initial_flow,
    reach_level,
    upstream,
):
    tile_local, mem_local, hour_feat = forcing.shape
    part_count = lax.axis_size("basin")
    basin_local = initial_flow.shape[0]
    reaches = reach_level.shape[0]
    groups = part_count // mem_local
    rows = reaches // groups
    in_kernel = reaches <= KERNEL_REACHES and rows == LANES
    tables = (celerity[None], storage[None], reach_level[None], upstream.T) if in_kernel else ()

    vmem = pl.BlockSpec(memory_space=pltpu.VMEM)
    params = pltpu.CompilerParams(vmem_limit_bytes=48 << 20)
    operands = (forcing, tile_weight.T, tile_part.T, tile_slot.T, initial_flow.T)
    send = pl.pallas_call(
        functools.partial(pack_kernel, basin_local),
        out_shape=jax.ShapeDtypeStruct(
            (part_count, tile_local + tile_local // 2 + EXTRAS, LANES), jnp.bfloat16
        ),
        in_specs=[pl.BlockSpec(memory_space=pltpu.HBM)] * len(operands),
        out_specs=vmem,
        scratch_shapes=[pltpu.VMEM(x.shape, x.dtype) for x in operands]
        + [pltpu.SemaphoreType.DMA((len(operands),))],
        compiler_params=pltpu.CompilerParams(vmem_limit_bytes=60 << 20),
    )(*operands)
    arrived = lax.all_to_all(send, "basin", split_axis=0, concat_axis=0, tiled=True)
    sources = min(part_count, 8)
    units = w_encoder.shape[0]
    scale = jnp.where(jnp.arange(4 * units) // units == 2, 1.0, 0.5).astype(jnp.float32)
    shared = (b_encoder[None] * scale, b_decoder[None] * scale, w_output[None], *tables)
    blank = jnp.zeros((INPUT_ROW - sum(x.shape[0] for x in shared), 1), jnp.float32)
    small = stacked(INPUT_ROW + FEAT, 4 * units, (*shared, blank, w_input * scale))
    w_encoder = (w_encoder * scale).astype(jnp.bfloat16)
    w_decoder = (w_decoder * scale).astype(jnp.bfloat16)
    lateral = pl.pallas_call(
        functools.partial(lstm_kernel, (hour_feat, tile_local, basin_local, groups, sources)),
        out_shape=jax.ShapeDtypeStruct((8, rows), jnp.float32),
        in_specs=[vmem] * 4,
        out_specs=vmem,
        compiler_params=params,
    )(arrived, small, w_encoder, w_decoder)
    axes = ("member", "basin")
    world = lax.axis_size("member") * part_count
    copies = jnp.broadcast_to(lateral.astype(CARRIED)[None], (world,) + lateral.shape)
    gathered = lax.all_to_all(copies, axes, split_axis=0, concat_axis=0, tiled=True)
    gathered = gathered.astype(jnp.float32)
    if not in_kernel:
        return route_plain(gathered, upstream, reach_level, celerity, storage, mem_local, basin_local)
    discharge, ensemble = pl.pallas_call(
        functools.partial(route_kernel, mem_local, basin_local, reaches),
        out_shape=(
            jax.ShapeDtypeStruct((DEC, mem_local, basin_local), jnp.float32),
            jax.ShapeDtypeStruct((DEC, basin_local), jnp.float32),
        ),
        in_specs=[vmem] * 2,
        out_specs=(vmem, vmem),
        compiler_params=params,
    )(gathered.reshape(world * 8, rows), small)
    return jnp.transpose(discharge, (2, 1, 0)), ensemble.T


def solution(mesh):
    placed = (
        P("basin", "member", None),
        P("basin", None),
        P("basin", None),
        P("basin", None),
        P(),
        P(),
        P(),
        P(),
        P(),
        P(),
        P(),
        P(),
        P("basin", "member"),
        P(),
        P(),
    )
    return jax.shard_map(
        on_device,
        mesh=mesh,
        in_specs=placed,
        out_specs=(P("basin", "member", None), P("basin", None)),
        check_vma=False,
    )
```

```python
import functools

import jax
import jax.numpy as jnp
from jax import lax
from jax.experimental import pallas as pl
from jax.experimental.pallas import tpu as pltpu
from jax.sharding import PartitionSpec as P

FEAT = 8
DEC = 6
TOP = 2
LEVELS = 4
NEWTON = 4
BETA = 0.6
LANES = 128
KERNEL_REACHES = 512
EXTRAS = 8
CARRIED = jnp.float16
HALF_STEP = 2.0**11
INPUT_ROW = 16

dot = functools.partial(jnp.dot, preferred_element_type=jnp.float32)


def cell_update(gate_sum, memory_cell):
    units = memory_cell.shape[-1]
    input_gate = 0.5 * jnp.tanh(gate_sum[:, :units]) + 0.5
    candidate = jnp.tanh(gate_sum[:, 2 * units : 3 * units])
    kept = 0.5 * memory_cell
    fresh = kept + input_gate * candidate
    memory_cell = jnp.tanh(gate_sum[:, units : 2 * units]) * kept + fresh
    output_gate = 0.5 * jnp.tanh(gate_sum[:, 3 * units :]) + 0.5
    hidden = (output_gate * jnp.tanh(memory_cell)).astype(jnp.bfloat16)
    return hidden, memory_cell


def stacked(height, width, parts):
    total = jnp.zeros((height, width), jnp.float32)
    at = 0
    for rows in parts:
        count, length = rows.shape
        total = total + jnp.pad(
            rows.astype(jnp.float32), ((at, height - at - count), (0, width - length))
        )
        at += count
    return total


def pack_kernel(basin_local, *refs):
    count = len(refs) // 2 - 1
    sources, send, held, semaphores = refs[:count], refs[count], refs[count + 1 : -1], refs[-1]
    copies = [
        pltpu.make_async_copy(source, target, semaphores.at[i])
        for i, (source, target) in enumerate(zip(sources, held, strict=True))
    ]
    for copy in copies:
        copy.start()
    for copy in copies:
        copy.wait()
    forcing, weight, part, slot, flow = held
    tile_local, members, width = forcing.shape
    groups = send.shape[0] // members
    half = tile_local // 2

    def pieces(values):
        high = values.astype(jnp.bfloat16).astype(jnp.float32)
        rest = values - high
        middle = rest.astype(jnp.bfloat16).astype(jnp.float32)
        return [high, middle, rest - middle]

    def side_by_side(rows):
        return jnp.concatenate([rows[entry : entry + 1] for entry in range(TOP)], axis=1)

    common = pieces(side_by_side(weight[...]))
    common += [side_by_side(part[...].astype(jnp.float32)), side_by_side(slot[...].astype(jnp.float32))]
    owners = LANES // basin_local
    lane = lax.broadcasted_iota(jnp.int32, (1, LANES), 1)
    mine = lane // basin_local == lax.rem(lax.axis_index("basin"), owners)
    for member in range(members):
        tiles = forcing[:, member, :]
        first = tiles[:, :LANES]
        second = jnp.concatenate([tiles[:half, LANES:], tiles[half:, LANES:]], axis=1)
        own_flow = flow[member : member + 1, :]
        own_flow = jnp.concatenate([own_flow] * owners, axis=1)
        rows = common + pieces(jnp.where(mine, own_flow, 0.0))
        extras = jnp.concatenate(rows, axis=0).astype(jnp.bfloat16)
        for group in range(groups):
            device = member * groups + group
            send[device, :tile_local, :] = first
            send[device, tile_local : tile_local + half, :] = second
            send[device, tile_local + half :, :] = extras


def encode(values):
    spread = values * (2.0**13 + 1.0)
    rounded = spread - (spread - values)
    place = (values - rounded) / jnp.maximum(rounded, 1e-30)
    digits = jnp.clip(jnp.floor(place * (1.5 * HALF_STEP) + 0.5), -1.0, 1.0)
    total = digits[0:1]
    for k in range(1, values.shape[0]):
        total = total + 3.0**k * digits[k : k + 1]
    return jnp.concatenate([rounded, total], axis=0)


def decode(rows):
    *rounded, total = rows
    values = []
    for row in rounded:
        above = jnp.floor(total * (1.0 / 3.0) + 0.5)
        values.append(row + row * ((total - 3.0 * above) * (1.0 / (1.5 * HALF_STEP))))
        total = above
    return values


def lstm_kernel(
    shape, arrived, small, w_encoder, w_decoder, out
):
    hour_feat, tile_local, basin_local, groups, sources = shape
    hours = hour_feat // FEAT
    devices = arrived.shape[0]
    rows = out.shape[1]
    units = w_encoder.shape[0]
    half = lax.rem(lax.axis_index("basin"), groups)
    first = (half * rows).astype(jnp.float32)
    folded = tile_local // 2
    extra_at = tile_local + folded

    def add_sources(chunk, total):
        block = arrived[pl.ds(chunk * sources, sources)].astype(jnp.float32)
        extras = block[:, extra_at:, :]
        weight = extras[:, 0] + extras[:, 1] + extras[:, 2]
        basin = extras[:, 3] * basin_local + extras[:, 4] - first
        weight = weight.T
        row_of = lax.broadcasted_iota(jnp.int32, (rows, TOP * tile_local), 0).astype(jnp.float32)
        picked, terms = [], []
        for source in range(sources):
            picked.append(jnp.where(row_of == basin[source : source + 1], 1.0, 0.0).astype(jnp.bfloat16))
            second = block[source, tile_local:extra_at, :]
            second = jnp.concatenate([second, pltpu.roll(second, LANES // 2, 1)], axis=0)
            tiles = jnp.concatenate([block[source, :tile_local, :], second], axis=1)
            for entry in range(TOP):
                column = weight[entry * tile_local : (entry + 1) * tile_local, source : source + 1]
                terms.append((column * tiles).astype(jnp.bfloat16))
        return total + dot(jnp.concatenate(picked, axis=1), jnp.concatenate(terms, axis=0))

    total = jnp.zeros((rows, 2 * LANES), jnp.float32)
    if devices == sources:
        total = add_sources(0, total)
    else:
        total = lax.fori_loop(0, devices // sources, add_sources, total)
    inputs = total.astype(jnp.bfloat16)

    owners = rows // basin_local
    flow = arrived[pl.ds(half * owners, owners), extra_at:, :].astype(jnp.float32)
    flow = jnp.sum(flow, axis=0)
    results = []
    b_encoder, b_decoder = small[0:1, : 4 * units], small[1:2, : 4 * units]
    w_input = small[INPUT_ROW : INPUT_ROW + FEAT, : 4 * units].astype(jnp.bfloat16)
    w_output = jnp.broadcast_to(small[2:3, :units], (8, units)).astype(jnp.bfloat16)

    hidden = jnp.zeros((rows, units), jnp.bfloat16)
    memory_cell = jnp.zeros((rows, units), jnp.float32)
    ahead = dot(inputs[:, :FEAT], w_input) + b_encoder
    for hour in range(hours):
        gate_sum = ahead + dot(hidden, w_encoder[...]) if hour else ahead
        if hour + 1 < hours:
            ahead = dot(inputs[:, (hour + 1) * FEAT : (hour + 2) * FEAT], w_input) + b_encoder
        hidden, memory_cell = cell_update(gate_sum, memory_cell)

    def runoff(state):
        sums = lax.dot_general(
            w_output, state, (((1,), (1,)), ((), ())), preferred_element_type=jnp.float32
        )[0:1]
        return jnp.maximum(sums, 0.0) + jnp.log(1.0 + jnp.exp(-jnp.abs(sums)))

    for hour in range(DEC):
        gate_sum = dot(hidden, w_decoder[...]) + b_decoder
        if hour:
            results.append(runoff(hidden))
        hidden, memory_cell = cell_update(gate_sum, memory_cell)
    results.append(runoff(hidden))
    results.append(flow[5:6] + flow[6:7] + flow[7:8])
    out[...] = encode(jnp.concatenate(results, axis=0))


def power(flow):
    return jnp.exp(BETA * jnp.log(flow))


def route_kernel(member_local, basin_local, reaches, gathered, small, discharge, ensemble):
    celerity, storage, level_row = small[3:4, :reaches], small[4:5, :reaches], small[5:6, :reaches]
    upstream = small[6:10, :reaches]
    halves = reaches // LANES
    per_member = halves * 8
    members = gathered.shape[0] // per_member
    shape = (members, LANES)

    def spread(row):
        return [jnp.broadcast_to(row[:, h * LANES : (h + 1) * LANES], shape) for h in range(halves)]

    def pick(parts, index):
        out = None
        for h, part in enumerate(parts):
            value = jnp.take_along_axis(part, index & (LANES - 1), axis=1)
            out = value if out is None else jnp.where(index >= h * LANES, value, out)
        return out

    level_parts = spread(level_row.astype(jnp.int32))
    levels = jnp.concatenate(level_parts, axis=1)
    sources, lags = [], []
    for entry in range(upstream.shape[0]):
        named = spread(upstream[entry : entry + 1, :].astype(jnp.int32))
        index = [jnp.maximum(x, 0) for x in named]
        sources.append(index)
        lags.append(
            [jnp.where(x < 0, 0, level - pick(level_parts, i)) for x, level, i in zip(named, level_parts, index, strict=True)]
        )

    def handed_on(flow):
        parts = [flow[:, h * LANES : (h + 1) * LANES] for h in range(halves)]
        sums = [[jnp.zeros(shape, jnp.float32)] * halves for _ in range(LEVELS - 1)]
        for index, lag in zip(sources, lags, strict=True):
            for h in range(halves):
                value = pick(parts, index[h])
                for k in range(LEVELS - 1):
                    sums[k][h] = sums[k][h] + jnp.where(lag[h] == k + 1, value, 0.0)
        return [jnp.concatenate(x, axis=1) for x in sums]

    speed_rate = jnp.broadcast_to(celerity, (members, reaches))
    store_rate = jnp.broadcast_to(storage, (members, reaches))

    def row(k):
        return jnp.concatenate(
            [gathered[pl.ds(h * 8 + k, members, stride=per_member), :] for h in range(halves)], axis=1
        )

    *lateral, current = decode([row(k) for k in range(8)])
    powered = power(current)
    series = [jnp.zeros((members, reaches), jnp.float32) for _ in range(DEC)]
    given = []
    for step in range(DEC + LEVELS - 1):
        target = store_rate * powered
        for level in range(LEVELS):
            hour = step - level
            if 0 <= hour < DEC:
                target = jnp.where(levels == level, target + lateral[hour], target)
        for k in range(LEVELS - 1):
            if step - 1 - k >= 0:
                target = target + speed_rate * given[step - 1 - k][k]
        flow, flow_power = current, powered
        for _ in range(NEWTON):
            slope = speed_rate * flow + BETA * store_rate * flow_power
            reached = jnp.maximum(target - (1.0 - BETA) * store_rate * flow_power, 0.5 * slope)
            flow = flow * (reached / slope)
            flow_power = flow_power * jnp.exp(BETA * (jnp.log(reached) - jnp.log(slope)))
        active = (levels <= step) & (levels > step - DEC)
        current = jnp.where(active, flow, current)
        powered = jnp.where(active, flow_power, powered)
        given.append(handed_on(current) if step + 1 < DEC + LEVELS - 1 else None)
        for level in range(LEVELS):
            hour = step - level
            if 0 <= hour < DEC:
                series[hour] = jnp.where(levels == level, flow, series[hour])
    column = lax.axis_index("basin") * basin_local
    mine = lax.axis_index("member")
    block = column // LANES
    shift = lax.rem(LANES - lax.rem(column, LANES), LANES)
    for hour in range(DEC):
        value = series[hour]
        picked = value[:, 0:LANES]
        for h in range(1, halves):
            picked = jnp.where(block == h, value[:, h * LANES : (h + 1) * LANES], picked)
        picked = pltpu.roll(picked, shift, 1)
        kept = picked[0:member_local]
        for q in range(1, members // member_local):
            kept = jnp.where(mine == q, picked[q * member_local : (q + 1) * member_local], kept)
        discharge[hour] = kept[:, 0:basin_local]
        mean = jnp.sum(picked, axis=0, keepdims=True) / members
        ensemble[hour : hour + 1, :] = mean[:, 0:basin_local]


def route_plain(gathered, upstream, reach_level, celerity, storage, mem_local, basin_local):
    reaches = reach_level.shape[0]
    members = gathered.shape[0] * gathered.shape[2] // reaches
    whole = gathered.reshape(members, -1, gathered.shape[1], gathered.shape[2])
    whole = jnp.transpose(whole, (1, 3, 0, 2)).reshape(reaches, members, gathered.shape[1])
    *lateral, initial = decode([whole[:, :, k] for k in range(8)])
    lateral = jnp.stack(lateral, axis=2)
    speed_rate, store_rate = celerity[:, None], storage[:, None]
    up_index = jnp.where(upstream < 0, reaches, upstream)
    outflow = jnp.zeros_like(lateral)
    for level_now in range(LEVELS):
        padded = jnp.concatenate([outflow, jnp.zeros_like(outflow[:1])], axis=0)
        inflow = padded[up_index[:, 0]]
        for entry in range(1, up_index.shape[1]):
            inflow = inflow + padded[up_index[:, entry]]
        flow = initial
        hours = []
        for hour in range(DEC):
            flow_power = flow**BETA
            target = speed_rate * inflow[:, :, hour] + store_rate * flow_power + lateral[:, :, hour]
            for _ in range(NEWTON):
                flow_power = flow**BETA
                ratio = (target - (1.0 - BETA) * store_rate * flow_power) / (
                    speed_rate * flow + BETA * store_rate * flow_power
                )
                flow = flow * jnp.maximum(ratio, 0.5)
            hours.append(flow)
        routed = jnp.stack(hours, axis=2)
        outflow = jnp.where((reach_level == level_now)[:, None, None], routed, outflow)
    ensemble = jnp.sum(outflow, axis=1) / members
    first_row = lax.axis_index("basin") * basin_local
    mine = lax.dynamic_slice_in_dim(outflow, first_row, basin_local, 0)
    mine = lax.dynamic_slice_in_dim(mine, lax.axis_index("member") * mem_local, mem_local, 1)
    return mine, lax.dynamic_slice_in_dim(ensemble, first_row, basin_local, 0)


def on_device(
    forcing,
    tile_part,
    tile_slot,
    tile_weight,
    w_input,
    w_encoder,
    b_encoder,
    w_decoder,
    b_decoder,
    w_output,
    celerity,
    storage,
    initial_flow,
    reach_level,
    upstream,
):
    tile_local, mem_local, hour_feat = forcing.shape
    part_count = lax.axis_size("basin")
    basin_local = initial_flow.shape[0]
    reaches = reach_level.shape[0]
    groups = part_count // mem_local
    rows = reaches // groups
    in_kernel = reaches <= KERNEL_REACHES and rows == LANES
    tables = (celerity[None], storage[None], reach_level[None], upstream.T) if in_kernel else ()

    vmem = pl.BlockSpec(memory_space=pltpu.VMEM)
    params = pltpu.CompilerParams(vmem_limit_bytes=48 << 20)
    operands = (forcing, tile_weight.T, tile_part.T, tile_slot.T, initial_flow.T)
    send = pl.pallas_call(
        functools.partial(pack_kernel, basin_local),
        out_shape=jax.ShapeDtypeStruct(
            (part_count, tile_local + tile_local // 2 + EXTRAS, LANES), jnp.bfloat16
        ),
        in_specs=[pl.BlockSpec(memory_space=pltpu.HBM)] * len(operands),
        out_specs=vmem,
        scratch_shapes=[pltpu.VMEM(x.shape, x.dtype) for x in operands]
        + [pltpu.SemaphoreType.DMA((len(operands),))],
        compiler_params=pltpu.CompilerParams(vmem_limit_bytes=60 << 20),
    )(*operands)
    arrived = lax.all_to_all(send, "basin", split_axis=0, concat_axis=0, tiled=True)
    sources = min(part_count, 8)
    units = w_encoder.shape[0]
    scale = jnp.where(jnp.arange(4 * units) // units == 2, 1.0, 0.5).astype(jnp.float32)
    shared = (b_encoder[None] * scale, b_decoder[None] * scale, w_output[None], *tables)
    blank = jnp.zeros((INPUT_ROW - sum(x.shape[0] for x in shared), 1), jnp.float32)
    small = stacked(INPUT_ROW + FEAT, 4 * units, (*shared, blank, w_input * scale))
    w_encoder = (w_encoder * scale).astype(jnp.bfloat16)
    w_decoder = (w_decoder * scale).astype(jnp.bfloat16)
    lateral = pl.pallas_call(
        functools.partial(lstm_kernel, (hour_feat, tile_local, basin_local, groups, sources)),
        out_shape=jax.ShapeDtypeStruct((8, rows), jnp.float32),
        in_specs=[vmem] * 4,
        out_specs=vmem,
        compiler_params=params,
    )(arrived, small, w_encoder, w_decoder)
    axes = ("member", "basin")
    world = lax.axis_size("member") * part_count
    copies = jnp.broadcast_to(lateral.astype(CARRIED)[None], (world,) + lateral.shape)
    gathered = lax.all_to_all(copies, axes, split_axis=0, concat_axis=0, tiled=True)
    gathered = gathered.astype(jnp.float32)
    if not in_kernel:
        return route_plain(gathered, upstream, reach_level, celerity, storage, mem_local, basin_local)
    discharge, ensemble = pl.pallas_call(
        functools.partial(route_kernel, mem_local, basin_local, reaches),
        out_shape=(
            jax.ShapeDtypeStruct((DEC, mem_local, basin_local), jnp.float32),
            jax.ShapeDtypeStruct((DEC, basin_local), jnp.float32),
        ),
        in_specs=[vmem] * 2,
        out_specs=(vmem, vmem),
        compiler_params=params,
    )(gathered.reshape(world * 8, rows), small)
    return jnp.transpose(discharge, (2, 1, 0)), ensemble.T


def solution(mesh):
    placed = (
        P("basin", "member", None),
        P("basin", None),
        P("basin", None),
        P("basin", None),
        P(),
        P(),
        P(),
        P(),
        P(),
        P(),
        P(),
        P(),
        P("basin", "member"),
        P(),
        P(),
    )
    return jax.shard_map(
        on_device,
        mesh=mesh,
        in_specs=placed,
        out_specs=(P("basin", "member", None), P("basin", None)),
        check_vma=False,
    )
```

```python
import functools

import jax
import jax.numpy as jnp
from jax import lax
from jax.experimental import pallas as pl
from jax.experimental.pallas import tpu as pltpu
from jax.sharding import PartitionSpec as P

FEAT = 8
DEC = 6
TOP = 2
LEVELS = 4
NEWTON = 4
BETA = 0.6
LANES = 128
KERNEL_REACHES = 512
EXTRAS = 8
CARRIED = jnp.float16
HALF_STEP = 2.0**11
INPUT_ROW = 16

dot = functools.partial(jnp.dot, preferred_element_type=jnp.float32)


def cell_update(gate_sum, memory_cell):
    units = memory_cell.shape[-1]
    input_gate = 0.5 * jnp.tanh(gate_sum[:, :units]) + 0.5
    candidate = jnp.tanh(gate_sum[:, 2 * units : 3 * units])
    kept = 0.5 * memory_cell
    fresh = kept + input_gate * candidate
    memory_cell = jnp.tanh(gate_sum[:, units : 2 * units]) * kept + fresh
    output_gate = 0.5 * jnp.tanh(gate_sum[:, 3 * units :]) + 0.5
    hidden = (output_gate * jnp.tanh(memory_cell)).astype(jnp.bfloat16)
    return hidden, memory_cell


def stacked(height, width, parts):
    total = jnp.zeros((height, width), jnp.float32)
    at = 0
    for rows in parts:
        count, length = rows.shape
        total = total + jnp.pad(
            rows.astype(jnp.float32), ((at, height - at - count), (0, width - length))
        )
        at += count
    return total


def position(device, member, count):
    place = jnp.where(device < count // 2, 2 * device, 2 * (count - 1 - device) + 1)
    place = jnp.where(lax.rem(member, 2) == 1, count - 1 - place, place)
    return jnp.where(lax.rem(member // 2, 2) == 1, lax.rem(place + count // 2, count), place)


def exchange_groups(count, members):
    ends = [x for pair in zip(range(count // 2), range(count - 1, count // 2 - 1, -1), strict=True) for x in pair]
    groups = []
    for member in range(members):
        order = ends[::-1] if member % 2 else ends
        if member // 2 % 2:
            order = order[count // 2 :] + order[: count // 2]
        groups.append([device * members + member for device in order])
    return groups


def pack_kernel(basin_local, *refs):
    count = len(refs) // 2 - 1
    sources, send, held, semaphores = refs[:count], refs[count], refs[count + 1 : -1], refs[-1]
    copies = [
        pltpu.make_async_copy(source, target, semaphores.at[i])
        for i, (source, target) in enumerate(zip(sources, held, strict=True))
    ]
    for copy in copies:
        copy.start()
    for copy in copies:
        copy.wait()
    forcing, weight, part, slot, flow = held
    tile_local, members, width = forcing.shape
    groups = send.shape[0] // members
    half = tile_local // 2

    def pieces(values):
        high = values.astype(jnp.bfloat16).astype(jnp.float32)
        rest = values - high
        middle = rest.astype(jnp.bfloat16).astype(jnp.float32)
        return [high, middle, rest - middle]

    def side_by_side(rows):
        return jnp.concatenate([rows[entry : entry + 1] for entry in range(TOP)], axis=1)

    common = pieces(side_by_side(weight[...]))
    common += [side_by_side(part[...].astype(jnp.float32)), side_by_side(slot[...].astype(jnp.float32))]
    owners = LANES // basin_local
    lane = lax.broadcasted_iota(jnp.int32, (1, LANES), 1)
    mine = lane // basin_local == lax.rem(lax.axis_index("basin"), owners)
    mine_member = lax.axis_index("member")
    for member in range(members):
        tiles = forcing[:, member, :]
        first = tiles[:, :LANES]
        second = jnp.concatenate([tiles[:half, LANES:], tiles[half:, LANES:]], axis=1)
        own_flow = flow[member : member + 1, :]
        own_flow = jnp.concatenate([own_flow] * owners, axis=1)
        rows = common + pieces(jnp.where(mine, own_flow, 0.0))
        extras = jnp.concatenate(rows, axis=0).astype(jnp.bfloat16)
        for group in range(groups):
            place = position(member * groups + group, mine_member, send.shape[0])
            send[place, :tile_local, :] = first
            send[place, tile_local : tile_local + half, :] = second
            send[place, tile_local + half :, :] = extras


def encode(values):
    spread = values * (2.0**13 + 1.0)
    rounded = spread - (spread - values)
    place = (values - rounded) / jnp.maximum(rounded, 1e-30)
    digits = jnp.clip(jnp.floor(place * (1.5 * HALF_STEP) + 0.5), -1.0, 1.0)
    total = digits[0:1]
    for k in range(1, values.shape[0]):
        total = total + 3.0**k * digits[k : k + 1]
    return jnp.concatenate([rounded, total], axis=0)


def decode(rows):
    *rounded, total = rows
    values = []
    for row in rounded:
        above = jnp.floor(total * (1.0 / 3.0) + 0.5)
        values.append(row + row * ((total - 3.0 * above) * (1.0 / (1.5 * HALF_STEP))))
        total = above
    return values


def lstm_kernel(
    shape, arrived, small, w_encoder, w_decoder, out
):
    hour_feat, tile_local, basin_local, groups, sources = shape
    hours = hour_feat // FEAT
    devices = arrived.shape[0]
    rows = out.shape[1]
    units = w_encoder.shape[0]
    half = lax.rem(lax.axis_index("basin"), groups)
    first = (half * rows).astype(jnp.float32)
    folded = tile_local // 2
    extra_at = tile_local + folded

    def add_sources(chunk, total):
        block = arrived[pl.ds(chunk * sources, sources)].astype(jnp.float32)
        extras = block[:, extra_at:, :]
        weight = extras[:, 0] + extras[:, 1] + extras[:, 2]
        basin = extras[:, 3] * basin_local + extras[:, 4] - first
        weight = weight.T
        row_of = lax.broadcasted_iota(jnp.int32, (rows, TOP * tile_local), 0).astype(jnp.float32)
        picked, terms = [], []
        for source in range(sources):
            picked.append(jnp.where(row_of == basin[source : source + 1], 1.0, 0.0).astype(jnp.bfloat16))
            second = block[source, tile_local:extra_at, :]
            second = jnp.concatenate([second, pltpu.roll(second, LANES // 2, 1)], axis=0)
            tiles = jnp.concatenate([block[source, :tile_local, :], second], axis=1)
            for entry in range(TOP):
                column = weight[entry * tile_local : (entry + 1) * tile_local, source : source + 1]
                terms.append((column * tiles).astype(jnp.bfloat16))
        return total + dot(jnp.concatenate(picked, axis=1), jnp.concatenate(terms, axis=0))

    total = jnp.zeros((rows, 2 * LANES), jnp.float32)
    if devices == sources:
        total = add_sources(0, total)
    else:
        total = lax.fori_loop(0, devices // sources, add_sources, total)
    inputs = total.astype(jnp.bfloat16)

    owners = rows // basin_local
    member = lax.axis_index("member")
    flow = jnp.zeros((EXTRAS, rows), jnp.float32)
    for owner in range(owners):
        place = position(half * owners + owner, member, devices)
        flow = flow + arrived[place, extra_at:, :].astype(jnp.float32)
    results = []
    b_encoder, b_decoder = small[0:1, : 4 * units], small[1:2, : 4 * units]
    w_input = small[INPUT_ROW : INPUT_ROW + FEAT, : 4 * units].astype(jnp.bfloat16)
    w_output = jnp.broadcast_to(small[2:3, :units], (8, units)).astype(jnp.bfloat16)

    hidden = jnp.zeros((rows, units), jnp.bfloat16)
    memory_cell = jnp.zeros((rows, units), jnp.float32)
    ahead = dot(inputs[:, :FEAT], w_input) + b_encoder
    for hour in range(hours):
        gate_sum = ahead + dot(hidden, w_encoder[...]) if hour else ahead
        if hour + 1 < hours:
            ahead = dot(inputs[:, (hour + 1) * FEAT : (hour + 2) * FEAT], w_input) + b_encoder
        hidden, memory_cell = cell_update(gate_sum, memory_cell)

    def runoff(state):
        sums = lax.dot_general(
            w_output, state, (((1,), (1,)), ((), ())), preferred_element_type=jnp.float32
        )[0:1]
        return jnp.maximum(sums, 0.0) + jnp.log(1.0 + jnp.exp(-jnp.abs(sums)))

    for hour in range(DEC):
        gate_sum = dot(hidden, w_decoder[...]) + b_decoder
        if hour:
            results.append(runoff(hidden))
        hidden, memory_cell = cell_update(gate_sum, memory_cell)
    results.append(runoff(hidden))
    results.append(flow[5:6] + flow[6:7] + flow[7:8])
    out[...] = encode(jnp.concatenate(results, axis=0))


def power(flow):
    return jnp.exp(BETA * jnp.log(flow))


def route_kernel(member_local, basin_local, reaches, gathered, small, discharge, ensemble):
    celerity, storage, level_row = small[3:4, :reaches], small[4:5, :reaches], small[5:6, :reaches]
    upstream = small[6:10, :reaches]
    halves = reaches // LANES
    per_member = halves * 8
    members = gathered.shape[0] // per_member
    shape = (members, LANES)

    def spread(row):
        return [jnp.broadcast_to(row[:, h * LANES : (h + 1) * LANES], shape) for h in range(halves)]

    def pick(parts, index):
        out = None
        for h, part in enumerate(parts):
            value = jnp.take_along_axis(part, index & (LANES - 1), axis=1)
            out = value if out is None else jnp.where(index >= h * LANES, value, out)
        return out

    level_parts = spread(level_row.astype(jnp.int32))
    levels = jnp.concatenate(level_parts, axis=1)
    sources, lags = [], []
    for entry in range(upstream.shape[0]):
        named = spread(upstream[entry : entry + 1, :].astype(jnp.int32))
        index = [jnp.maximum(x, 0) for x in named]
        sources.append(index)
        lags.append(
            [jnp.where(x < 0, 0, level - pick(level_parts, i)) for x, level, i in zip(named, level_parts, index, strict=True)]
        )

    def handed_on(flow):
        parts = [flow[:, h * LANES : (h + 1) * LANES] for h in range(halves)]
        sums = [[jnp.zeros(shape, jnp.float32)] * halves for _ in range(LEVELS - 1)]
        for index, lag in zip(sources, lags, strict=True):
            for h in range(halves):
                value = pick(parts, index[h])
                for k in range(LEVELS - 1):
                    sums[k][h] = sums[k][h] + jnp.where(lag[h] == k + 1, value, 0.0)
        return [jnp.concatenate(x, axis=1) for x in sums]

    speed_rate = jnp.broadcast_to(celerity, (members, reaches))
    store_rate = jnp.broadcast_to(storage, (members, reaches))

    def row(k):
        return jnp.concatenate(
            [gathered[pl.ds(h * 8 + k, members, stride=per_member), :] for h in range(halves)], axis=1
        )

    *lateral, current = decode([row(k) for k in range(8)])
    powered = power(current)
    series = [jnp.zeros((members, reaches), jnp.float32) for _ in range(DEC)]
    given = []
    for step in range(DEC + LEVELS - 1):
        target = store_rate * powered
        for level in range(LEVELS):
            hour = step - level
            if 0 <= hour < DEC:
                target = jnp.where(levels == level, target + lateral[hour], target)
        for k in range(LEVELS - 1):
            if step - 1 - k >= 0:
                target = target + speed_rate * given[step - 1 - k][k]
        flow, flow_power = current, powered
        for _ in range(NEWTON):
            slope = speed_rate * flow + BETA * store_rate * flow_power
            reached = jnp.maximum(target - (1.0 - BETA) * store_rate * flow_power, 0.5 * slope)
            flow = flow * (reached / slope)
            flow_power = flow_power * jnp.exp(BETA * (jnp.log(reached) - jnp.log(slope)))
        active = (levels <= step) & (levels > step - DEC)
        current = jnp.where(active, flow, current)
        powered = jnp.where(active, flow_power, powered)
        given.append(handed_on(current) if step + 1 < DEC + LEVELS - 1 else None)
        for level in range(LEVELS):
            hour = step - level
            if 0 <= hour < DEC:
                series[hour] = jnp.where(levels == level, flow, series[hour])
    column = lax.axis_index("basin") * basin_local
    mine = lax.axis_index("member")
    block = column // LANES
    shift = lax.rem(LANES - lax.rem(column, LANES), LANES)
    for hour in range(DEC):
        value = series[hour]
        picked = value[:, 0:LANES]
        for h in range(1, halves):
            picked = jnp.where(block == h, value[:, h * LANES : (h + 1) * LANES], picked)
        picked = pltpu.roll(picked, shift, 1)
        kept = picked[0:member_local]
        for q in range(1, members // member_local):
            kept = jnp.where(mine == q, picked[q * member_local : (q + 1) * member_local], kept)
        discharge[hour] = kept[:, 0:basin_local]
        mean = jnp.sum(picked, axis=0, keepdims=True) / members
        ensemble[hour : hour + 1, :] = mean[:, 0:basin_local]


def route_plain(gathered, upstream, reach_level, celerity, storage, mem_local, basin_local):
    reaches = reach_level.shape[0]
    members = gathered.shape[0] * gathered.shape[2] // reaches
    whole = gathered.reshape(members, -1, gathered.shape[1], gathered.shape[2])
    whole = jnp.transpose(whole, (1, 3, 0, 2)).reshape(reaches, members, gathered.shape[1])
    *lateral, initial = decode([whole[:, :, k] for k in range(8)])
    lateral = jnp.stack(lateral, axis=2)
    speed_rate, store_rate = celerity[:, None], storage[:, None]
    up_index = jnp.where(upstream < 0, reaches, upstream)
    outflow = jnp.zeros_like(lateral)
    for level_now in range(LEVELS):
        padded = jnp.concatenate([outflow, jnp.zeros_like(outflow[:1])], axis=0)
        inflow = padded[up_index[:, 0]]
        for entry in range(1, up_index.shape[1]):
            inflow = inflow + padded[up_index[:, entry]]
        flow = initial
        hours = []
        for hour in range(DEC):
            flow_power = flow**BETA
            target = speed_rate * inflow[:, :, hour] + store_rate * flow_power + lateral[:, :, hour]
            for _ in range(NEWTON):
                flow_power = flow**BETA
                ratio = (target - (1.0 - BETA) * store_rate * flow_power) / (
                    speed_rate * flow + BETA * store_rate * flow_power
                )
                flow = flow * jnp.maximum(ratio, 0.5)
            hours.append(flow)
        routed = jnp.stack(hours, axis=2)
        outflow = jnp.where((reach_level == level_now)[:, None, None], routed, outflow)
    ensemble = jnp.sum(outflow, axis=1) / members
    first_row = lax.axis_index("basin") * basin_local
    mine = lax.dynamic_slice_in_dim(outflow, first_row, basin_local, 0)
    mine = lax.dynamic_slice_in_dim(mine, lax.axis_index("member") * mem_local, mem_local, 1)
    return mine, lax.dynamic_slice_in_dim(ensemble, first_row, basin_local, 0)


def on_device(
    forcing,
    tile_part,
    tile_slot,
    tile_weight,
    w_input,
    w_encoder,
    b_encoder,
    w_decoder,
    b_decoder,
    w_output,
    celerity,
    storage,
    initial_flow,
    reach_level,
    upstream,
):
    tile_local, mem_local, hour_feat = forcing.shape
    part_count = lax.axis_size("basin")
    basin_local = initial_flow.shape[0]
    reaches = reach_level.shape[0]
    groups = part_count // mem_local
    rows = reaches // groups
    in_kernel = reaches <= KERNEL_REACHES and rows == LANES
    tables = (celerity[None], storage[None], reach_level[None], upstream.T) if in_kernel else ()

    vmem = pl.BlockSpec(memory_space=pltpu.VMEM)
    params = pltpu.CompilerParams(vmem_limit_bytes=48 << 20)
    operands = (forcing, tile_weight.T, tile_part.T, tile_slot.T, initial_flow.T)
    send = pl.pallas_call(
        functools.partial(pack_kernel, basin_local),
        out_shape=jax.ShapeDtypeStruct(
            (part_count, tile_local + tile_local // 2 + EXTRAS, LANES), jnp.bfloat16
        ),
        in_specs=[pl.BlockSpec(memory_space=pltpu.HBM)] * len(operands),
        out_specs=vmem,
        scratch_shapes=[pltpu.VMEM(x.shape, x.dtype) for x in operands]
        + [pltpu.SemaphoreType.DMA((len(operands),))],
        compiler_params=pltpu.CompilerParams(vmem_limit_bytes=60 << 20),
    )(*operands)
    arrived = lax.all_to_all(
        send,
        ("basin", "member"),
        split_axis=0,
        concat_axis=0,
        tiled=True,
        axis_index_groups=exchange_groups(part_count, lax.axis_size("member")),
    )
    sources = min(part_count, 8)
    units = w_encoder.shape[0]
    scale = jnp.where(jnp.arange(4 * units) // units == 2, 1.0, 0.5).astype(jnp.float32)
    shared = (b_encoder[None] * scale, b_decoder[None] * scale, w_output[None], *tables)
    blank = jnp.zeros((INPUT_ROW - sum(x.shape[0] for x in shared), 1), jnp.float32)
    small = stacked(INPUT_ROW + FEAT, 4 * units, (*shared, blank, w_input * scale))
    w_encoder = (w_encoder * scale).astype(jnp.bfloat16)
    w_decoder = (w_decoder * scale).astype(jnp.bfloat16)
    lateral = pl.pallas_call(
        functools.partial(lstm_kernel, (hour_feat, tile_local, basin_local, groups, sources)),
        out_shape=jax.ShapeDtypeStruct((8, rows), jnp.float32),
        in_specs=[vmem] * 4,
        out_specs=vmem,
        compiler_params=params,
    )(arrived, small, w_encoder, w_decoder)
    axes = ("member", "basin")
    world = lax.axis_size("member") * part_count
    copies = jnp.broadcast_to(lateral.astype(CARRIED)[None], (world,) + lateral.shape)
    gathered = lax.all_to_all(copies, axes, split_axis=0, concat_axis=0, tiled=True)
    gathered = gathered.astype(jnp.float32)
    if not in_kernel:
        return route_plain(gathered, upstream, reach_level, celerity, storage, mem_local, basin_local)
    discharge, ensemble = pl.pallas_call(
        functools.partial(route_kernel, mem_local, basin_local, reaches),
        out_shape=(
            jax.ShapeDtypeStruct((DEC, mem_local, basin_local), jnp.float32),
            jax.ShapeDtypeStruct((DEC, basin_local), jnp.float32),
        ),
        in_specs=[vmem] * 2,
        out_specs=(vmem, vmem),
        compiler_params=params,
    )(gathered.reshape(world * 8, rows), small)
    return jnp.transpose(discharge, (2, 1, 0)), ensemble.T


def solution(mesh):
    placed = (
        P("basin", "member", None),
        P("basin", None),
        P("basin", None),
        P("basin", None),
        P(),
        P(),
        P(),
        P(),
        P(),
        P(),
        P(),
        P(),
        P("basin", "member"),
        P(),
        P(),
    )
    return jax.shard_map(
        on_device,
        mesh=mesh,
        in_specs=placed,
        out_specs=(P("basin", "member", None), P("basin", None)),
        check_vma=False,
    )
```

```python
import functools

import jax
import jax.numpy as jnp
from jax import lax
from jax.experimental import pallas as pl
from jax.experimental.pallas import tpu as pltpu
from jax.sharding import PartitionSpec as P

FEAT = 8
DEC = 6
TOP = 2
LEVELS = 4
NEWTON = 4
BETA = 0.6
LANES = 128
KERNEL_REACHES = 512
EXTRAS = 8
CARRIED = jnp.float16
HALF_STEP = 2.0**11
INPUT_ROW = 16
ORDERS = (
    (7, 2, 5, 4, 6, 0, 1, 3),
    (5, 3, 2, 6, 1, 7, 0, 4),
    (7, 2, 1, 6, 5, 0, 4, 3),
    (5, 7, 3, 0, 4, 6, 2, 1),
)

dot = functools.partial(jnp.dot, preferred_element_type=jnp.float32)


def cell_update(gate_sum, memory_cell):
    units = memory_cell.shape[-1]
    input_gate = 0.5 * jnp.tanh(gate_sum[:, :units]) + 0.5
    candidate = jnp.tanh(gate_sum[:, 2 * units : 3 * units])
    kept = 0.5 * memory_cell
    fresh = kept + input_gate * candidate
    memory_cell = jnp.tanh(gate_sum[:, units : 2 * units]) * kept + fresh
    output_gate = 0.5 * jnp.tanh(gate_sum[:, 3 * units :]) + 0.5
    hidden = (output_gate * jnp.tanh(memory_cell)).astype(jnp.bfloat16)
    return hidden, memory_cell


def stacked(height, width, parts):
    total = jnp.zeros((height, width), jnp.float32)
    at = 0
    for rows in parts:
        count, length = rows.shape
        total = total + jnp.pad(
            rows.astype(jnp.float32), ((at, height - at - count), (0, width - length))
        )
        at += count
    return total


def position(device, member, count):
    if (lax.axis_size("member"), count) == (len(ORDERS), len(ORDERS[0])):
        place = jnp.int32(0)
        for index, order in enumerate(ORDERS):
            here = jnp.int32(0)
            for at, named in enumerate(order):
                here = jnp.where(device == named, at, here)
            place = jnp.where(member == index, here, place)
        return place
    place = jnp.where(device < count // 2, 2 * device, 2 * (count - 1 - device) + 1)
    place = jnp.where(lax.rem(member, 2) == 1, count - 1 - place, place)
    return jnp.where(lax.rem(member // 2, 2) == 1, lax.rem(place + count // 2, count), place)


def exchange_groups(count, members):
    ends = [x for pair in zip(range(count // 2), range(count - 1, count // 2 - 1, -1), strict=True) for x in pair]
    groups = []
    for member in range(members):
        order = ends[::-1] if member % 2 else ends
        if member // 2 % 2:
            order = order[count // 2 :] + order[: count // 2]
        if (members, count) == (len(ORDERS), len(ORDERS[0])):
            order = ORDERS[member]
        groups.append([device * members + member for device in order])
    return groups


def pack_kernel(basin_local, *refs):
    count = len(refs) // 2 - 1
    sources, send, held, semaphores = refs[:count], refs[count], refs[count + 1 : -1], refs[-1]
    copies = [
        pltpu.make_async_copy(source, target, semaphores.at[i])
        for i, (source, target) in enumerate(zip(sources, held, strict=True))
    ]
    for copy in copies:
        copy.start()
    for copy in copies:
        copy.wait()
    forcing, weight, part, slot, flow = held
    tile_local, members, width = forcing.shape
    groups = send.shape[0] // members
    half = tile_local // 2

    def pieces(values):
        high = values.astype(jnp.bfloat16).astype(jnp.float32)
        rest = values - high
        middle = rest.astype(jnp.bfloat16).astype(jnp.float32)
        return [high, middle, rest - middle]

    def side_by_side(rows):
        return jnp.concatenate([rows[entry : entry + 1] for entry in range(TOP)], axis=1)

    common = pieces(side_by_side(weight[...]))
    common += [side_by_side(part[...].astype(jnp.float32)), side_by_side(slot[...].astype(jnp.float32))]
    owners = LANES // basin_local
    lane = lax.broadcasted_iota(jnp.int32, (1, LANES), 1)
    mine = lane // basin_local == lax.rem(lax.axis_index("basin"), owners)
    mine_member = lax.axis_index("member")
    for member in range(members):
        tiles = forcing[:, member, :]
        first = tiles[:, :LANES]
        second = jnp.concatenate([tiles[:half, LANES:], tiles[half:, LANES:]], axis=1)
        own_flow = flow[member : member + 1, :]
        own_flow = jnp.concatenate([own_flow] * owners, axis=1)
        rows = common + pieces(jnp.where(mine, own_flow, 0.0))
        extras = jnp.concatenate(rows, axis=0).astype(jnp.bfloat16)
        for group in range(groups):
            place = position(member * groups + group, mine_member, send.shape[0])
            send[place, :tile_local, :] = first
            send[place, tile_local : tile_local + half, :] = second
            send[place, tile_local + half :, :] = extras


def encode(values):
    spread = values * (2.0**13 + 1.0)
    rounded = spread - (spread - values)
    place = (values - rounded) / jnp.maximum(rounded, 1e-30)
    digits = jnp.clip(jnp.floor(place * (1.5 * HALF_STEP) + 0.5), -1.0, 1.0)
    total = digits[0:1]
    for k in range(1, values.shape[0]):
        total = total + 3.0**k * digits[k : k + 1]
    return jnp.concatenate([rounded, total], axis=0)


def decode(rows):
    *rounded, total = rows
    values = []
    for row in rounded:
        above = jnp.floor(total * (1.0 / 3.0) + 0.5)
        values.append(row + row * ((total - 3.0 * above) * (1.0 / (1.5 * HALF_STEP))))
        total = above
    return values


def lstm_kernel(
    shape, arrived, small, w_encoder, w_decoder, out
):
    hour_feat, tile_local, basin_local, groups, sources = shape
    hours = hour_feat // FEAT
    devices = arrived.shape[0]
    rows = out.shape[1]
    units = w_encoder.shape[0]
    half = lax.rem(lax.axis_index("basin"), groups)
    first = (half * rows).astype(jnp.float32)
    folded = tile_local // 2
    extra_at = tile_local + folded

    def add_sources(chunk, total):
        block = arrived[pl.ds(chunk * sources, sources)].astype(jnp.float32)
        extras = block[:, extra_at:, :]
        weight = extras[:, 0] + extras[:, 1] + extras[:, 2]
        basin = extras[:, 3] * basin_local + extras[:, 4] - first
        weight = weight.T
        row_of = lax.broadcasted_iota(jnp.int32, (rows, TOP * tile_local), 0).astype(jnp.float32)
        picked, terms = [], []
        for source in range(sources):
            picked.append(jnp.where(row_of == basin[source : source + 1], 1.0, 0.0).astype(jnp.bfloat16))
            second = block[source, tile_local:extra_at, :]
            second = jnp.concatenate([second, pltpu.roll(second, LANES // 2, 1)], axis=0)
            tiles = jnp.concatenate([block[source, :tile_local, :], second], axis=1)
            for entry in range(TOP):
                column = weight[entry * tile_local : (entry + 1) * tile_local, source : source + 1]
                terms.append((column * tiles).astype(jnp.bfloat16))
        return total + dot(jnp.concatenate(picked, axis=1), jnp.concatenate(terms, axis=0))

    total = jnp.zeros((rows, 2 * LANES), jnp.float32)
    if devices == sources:
        total = add_sources(0, total)
    else:
        total = lax.fori_loop(0, devices // sources, add_sources, total)
    inputs = total.astype(jnp.bfloat16)

    owners = rows // basin_local
    member = lax.axis_index("member")
    flow = jnp.zeros((EXTRAS, rows), jnp.float32)
    for owner in range(owners):
        place = position(half * owners + owner, member, devices)
        flow = flow + arrived[place, extra_at:, :].astype(jnp.float32)
    results = []
    b_encoder, b_decoder = small[0:1, : 4 * units], small[1:2, : 4 * units]
    w_input = small[INPUT_ROW : INPUT_ROW + FEAT, : 4 * units].astype(jnp.bfloat16)
    w_output = jnp.broadcast_to(small[2:3, :units], (8, units)).astype(jnp.bfloat16)

    hidden = jnp.zeros((rows, units), jnp.bfloat16)
    memory_cell = jnp.zeros((rows, units), jnp.float32)
    ahead = dot(inputs[:, :FEAT], w_input) + b_encoder
    for hour in range(hours):
        gate_sum = ahead + dot(hidden, w_encoder[...]) if hour else ahead
        if hour + 1 < hours:
            ahead = dot(inputs[:, (hour + 1) * FEAT : (hour + 2) * FEAT], w_input) + b_encoder
        hidden, memory_cell = cell_update(gate_sum, memory_cell)

    def runoff(state):
        sums = lax.dot_general(
            w_output, state, (((1,), (1,)), ((), ())), preferred_element_type=jnp.float32
        )[0:1]
        return jnp.maximum(sums, 0.0) + jnp.log(1.0 + jnp.exp(-jnp.abs(sums)))

    for hour in range(DEC):
        gate_sum = dot(hidden, w_decoder[...]) + b_decoder
        if hour:
            results.append(runoff(hidden))
        hidden, memory_cell = cell_update(gate_sum, memory_cell)
    results.append(runoff(hidden))
    results.append(flow[5:6] + flow[6:7] + flow[7:8])
    out[...] = encode(jnp.concatenate(results, axis=0))


def power(flow):
    return jnp.exp(BETA * jnp.log(flow))


def route_kernel(member_local, basin_local, reaches, gathered, small, discharge, ensemble):
    celerity, storage, level_row = small[3:4, :reaches], small[4:5, :reaches], small[5:6, :reaches]
    upstream = small[6:10, :reaches]
    halves = reaches // LANES
    per_member = halves * 8
    members = gathered.shape[0] // per_member
    shape = (members, LANES)

    def spread(row):
        return [jnp.broadcast_to(row[:, h * LANES : (h + 1) * LANES], shape) for h in range(halves)]

    def pick(parts, index):
        out = None
        for h, part in enumerate(parts):
            value = jnp.take_along_axis(part, index & (LANES - 1), axis=1)
            out = value if out is None else jnp.where(index >= h * LANES, value, out)
        return out

    level_parts = spread(level_row.astype(jnp.int32))
    levels = jnp.concatenate(level_parts, axis=1)
    sources, lags = [], []
    for entry in range(upstream.shape[0]):
        named = spread(upstream[entry : entry + 1, :].astype(jnp.int32))
        index = [jnp.maximum(x, 0) for x in named]
        sources.append(index)
        lags.append(
            [jnp.where(x < 0, 0, level - pick(level_parts, i)) for x, level, i in zip(named, level_parts, index, strict=True)]
        )

    def handed_on(flow):
        parts = [flow[:, h * LANES : (h + 1) * LANES] for h in range(halves)]
        sums = [[jnp.zeros(shape, jnp.float32)] * halves for _ in range(LEVELS - 1)]
        for index, lag in zip(sources, lags, strict=True):
            for h in range(halves):
                value = pick(parts, index[h])
                for k in range(LEVELS - 1):
                    sums[k][h] = sums[k][h] + jnp.where(lag[h] == k + 1, value, 0.0)
        return [jnp.concatenate(x, axis=1) for x in sums]

    speed_rate = jnp.broadcast_to(celerity, (members, reaches))
    store_rate = jnp.broadcast_to(storage, (members, reaches))

    def row(k):
        return jnp.concatenate(
            [gathered[pl.ds(h * 8 + k, members, stride=per_member), :] for h in range(halves)], axis=1
        )

    *lateral, current = decode([row(k) for k in range(8)])
    powered = power(current)
    series = [jnp.zeros((members, reaches), jnp.float32) for _ in range(DEC)]
    given = []
    for step in range(DEC + LEVELS - 1):
        target = store_rate * powered
        for level in range(LEVELS):
            hour = step - level
            if 0 <= hour < DEC:
                target = jnp.where(levels == level, target + lateral[hour], target)
        for k in range(LEVELS - 1):
            if step - 1 - k >= 0:
                target = target + speed_rate * given[step - 1 - k][k]
        flow, flow_power = current, powered
        for _ in range(NEWTON):
            slope = speed_rate * flow + BETA * store_rate * flow_power
            reached = jnp.maximum(target - (1.0 - BETA) * store_rate * flow_power, 0.5 * slope)
            flow = flow * (reached / slope)
            flow_power = flow_power * jnp.exp(BETA * (jnp.log(reached) - jnp.log(slope)))
        active = (levels <= step) & (levels > step - DEC)
        current = jnp.where(active, flow, current)
        powered = jnp.where(active, flow_power, powered)
        given.append(handed_on(current) if step + 1 < DEC + LEVELS - 1 else None)
        for level in range(LEVELS):
            hour = step - level
            if 0 <= hour < DEC:
                series[hour] = jnp.where(levels == level, flow, series[hour])
    column = lax.axis_index("basin") * basin_local
    mine = lax.axis_index("member")
    block = column // LANES
    shift = lax.rem(LANES - lax.rem(column, LANES), LANES)
    for hour in range(DEC):
        value = series[hour]
        picked = value[:, 0:LANES]
        for h in range(1, halves):
            picked = jnp.where(block == h, value[:, h * LANES : (h + 1) * LANES], picked)
        picked = pltpu.roll(picked, shift, 1)
        kept = picked[0:member_local]
        for q in range(1, members // member_local):
            kept = jnp.where(mine == q, picked[q * member_local : (q + 1) * member_local], kept)
        discharge[hour] = kept[:, 0:basin_local]
        mean = jnp.sum(picked, axis=0, keepdims=True) / members
        ensemble[hour : hour + 1, :] = mean[:, 0:basin_local]


def route_plain(gathered, upstream, reach_level, celerity, storage, mem_local, basin_local):
    reaches = reach_level.shape[0]
    members = gathered.shape[0] * gathered.shape[2] // reaches
    whole = gathered.reshape(members, -1, gathered.shape[1], gathered.shape[2])
    whole = jnp.transpose(whole, (1, 3, 0, 2)).reshape(reaches, members, gathered.shape[1])
    *lateral, initial = decode([whole[:, :, k] for k in range(8)])
    lateral = jnp.stack(lateral, axis=2)
    speed_rate, store_rate = celerity[:, None], storage[:, None]
    up_index = jnp.where(upstream < 0, reaches, upstream)
    outflow = jnp.zeros_like(lateral)
    for level_now in range(LEVELS):
        padded = jnp.concatenate([outflow, jnp.zeros_like(outflow[:1])], axis=0)
        inflow = padded[up_index[:, 0]]
        for entry in range(1, up_index.shape[1]):
            inflow = inflow + padded[up_index[:, entry]]
        flow = initial
        hours = []
        for hour in range(DEC):
            flow_power = flow**BETA
            target = speed_rate * inflow[:, :, hour] + store_rate * flow_power + lateral[:, :, hour]
            for _ in range(NEWTON):
                flow_power = flow**BETA
                ratio = (target - (1.0 - BETA) * store_rate * flow_power) / (
                    speed_rate * flow + BETA * store_rate * flow_power
                )
                flow = flow * jnp.maximum(ratio, 0.5)
            hours.append(flow)
        routed = jnp.stack(hours, axis=2)
        outflow = jnp.where((reach_level == level_now)[:, None, None], routed, outflow)
    ensemble = jnp.sum(outflow, axis=1) / members
    first_row = lax.axis_index("basin") * basin_local
    mine = lax.dynamic_slice_in_dim(outflow, first_row, basin_local, 0)
    mine = lax.dynamic_slice_in_dim(mine, lax.axis_index("member") * mem_local, mem_local, 1)
    return mine, lax.dynamic_slice_in_dim(ensemble, first_row, basin_local, 0)


def on_device(
    forcing,
    tile_part,
    tile_slot,
    tile_weight,
    w_input,
    w_encoder,
    b_encoder,
    w_decoder,
    b_decoder,
    w_output,
    celerity,
    storage,
    initial_flow,
    reach_level,
    upstream,
):
    tile_local, mem_local, hour_feat = forcing.shape
    part_count = lax.axis_size("basin")
    basin_local = initial_flow.shape[0]
    reaches = reach_level.shape[0]
    groups = part_count // mem_local
    rows = reaches // groups
    in_kernel = reaches <= KERNEL_REACHES and rows == LANES
    tables = (celerity[None], storage[None], reach_level[None], upstream.T) if in_kernel else ()

    vmem = pl.BlockSpec(memory_space=pltpu.VMEM)
    params = pltpu.CompilerParams(vmem_limit_bytes=48 << 20)
    operands = (forcing, tile_weight.T, tile_part.T, tile_slot.T, initial_flow.T)
    send = pl.pallas_call(
        functools.partial(pack_kernel, basin_local),
        out_shape=jax.ShapeDtypeStruct(
            (part_count, tile_local + tile_local // 2 + EXTRAS, LANES), jnp.bfloat16
        ),
        in_specs=[pl.BlockSpec(memory_space=pltpu.HBM)] * len(operands),
        out_specs=vmem,
        scratch_shapes=[pltpu.VMEM(x.shape, x.dtype) for x in operands]
        + [pltpu.SemaphoreType.DMA((len(operands),))],
        compiler_params=pltpu.CompilerParams(vmem_limit_bytes=60 << 20),
    )(*operands)
    arrived = lax.all_to_all(
        send,
        ("basin", "member"),
        split_axis=0,
        concat_axis=0,
        tiled=True,
        axis_index_groups=exchange_groups(part_count, lax.axis_size("member")),
    )
    sources = min(part_count, 8)
    units = w_encoder.shape[0]
    scale = jnp.where(jnp.arange(4 * units) // units == 2, 1.0, 0.5).astype(jnp.float32)
    shared = (b_encoder[None] * scale, b_decoder[None] * scale, w_output[None], *tables)
    blank = jnp.zeros((INPUT_ROW - sum(x.shape[0] for x in shared), 1), jnp.float32)
    small = stacked(INPUT_ROW + FEAT, 4 * units, (*shared, blank, w_input * scale))
    w_encoder = (w_encoder * scale).astype(jnp.bfloat16)
    w_decoder = (w_decoder * scale).astype(jnp.bfloat16)
    lateral = pl.pallas_call(
        functools.partial(lstm_kernel, (hour_feat, tile_local, basin_local, groups, sources)),
        out_shape=jax.ShapeDtypeStruct((8, rows), jnp.float32),
        in_specs=[vmem] * 4,
        out_specs=vmem,
        compiler_params=params,
    )(arrived, small, w_encoder, w_decoder)
    axes = ("member", "basin")
    world = lax.axis_size("member") * part_count
    copies = jnp.broadcast_to(lateral.astype(CARRIED)[None], (world,) + lateral.shape)
    gathered = lax.all_to_all(copies, axes, split_axis=0, concat_axis=0, tiled=True)
    gathered = gathered.astype(jnp.float32)
    if not in_kernel:
        return route_plain(gathered, upstream, reach_level, celerity, storage, mem_local, basin_local)
    discharge, ensemble = pl.pallas_call(
        functools.partial(route_kernel, mem_local, basin_local, reaches),
        out_shape=(
            jax.ShapeDtypeStruct((DEC, mem_local, basin_local), jnp.float32),
            jax.ShapeDtypeStruct((DEC, basin_local), jnp.float32),
        ),
        in_specs=[vmem] * 2,
        out_specs=(vmem, vmem),
        compiler_params=params,
    )(gathered.reshape(world * 8, rows), small)
    return jnp.transpose(discharge, (2, 1, 0)), ensemble.T


def solution(mesh):
    placed = (
        P("basin", "member", None),
        P("basin", None),
        P("basin", None),
        P("basin", None),
        P(),
        P(),
        P(),
        P(),
        P(),
        P(),
        P(),
        P(),
        P("basin", "member"),
        P(),
        P(),
    )
    return jax.shard_map(
        on_device,
        mesh=mesh,
        in_specs=placed,
        out_specs=(P("basin", "member", None), P("basin", None)),
        check_vma=False,
    )
```

```python
import functools

import jax
import jax.numpy as jnp
from jax import lax
from jax.experimental import pallas as pl
from jax.experimental.pallas import tpu as pltpu
from jax.sharding import PartitionSpec as P

FEAT = 8
DEC = 6
TOP = 2
LEVELS = 4
NEWTON = 4
BETA = 0.6
LANES = 128
KERNEL_REACHES = 512
EXTRAS = 8
CARRIED = jnp.float16
HALF_STEP = 2.0**11
INPUT_ROW = 16
ORDERS = ((7, 2, 5, 4, 6, 0, 1, 3), (5, 3, 2, 6, 1, 7, 0, 4), (7, 2, 5, 4, 6, 0, 1, 3), (5, 3, 2, 6, 1, 7, 0, 4))

dot = functools.partial(jnp.dot, preferred_element_type=jnp.float32)


def cell_update(gate_sum, memory_cell):
    units = memory_cell.shape[-1]
    input_gate = 0.5 * jnp.tanh(gate_sum[:, :units]) + 0.5
    candidate = jnp.tanh(gate_sum[:, 2 * units : 3 * units])
    kept = 0.5 * memory_cell
    fresh = kept + input_gate * candidate
    memory_cell = jnp.tanh(gate_sum[:, units : 2 * units]) * kept + fresh
    output_gate = 0.5 * jnp.tanh(gate_sum[:, 3 * units :]) + 0.5
    hidden = (output_gate * jnp.tanh(memory_cell)).astype(jnp.bfloat16)
    return hidden, memory_cell


def stacked(height, width, parts):
    total = jnp.zeros((height, width), jnp.float32)
    at = 0
    for rows in parts:
        count, length = rows.shape
        total = total + jnp.pad(
            rows.astype(jnp.float32), ((at, height - at - count), (0, width - length))
        )
        at += count
    return total


def position(device, member, count):
    if (lax.axis_size("member"), count) == (len(ORDERS), len(ORDERS[0])):
        place = jnp.int32(0)
        for index, order in enumerate(ORDERS):
            here = jnp.int32(0)
            for at, named in enumerate(order):
                here = jnp.where(device == named, at, here)
            place = jnp.where(member == index, here, place)
        return place
    place = jnp.where(device < count // 2, 2 * device, 2 * (count - 1 - device) + 1)
    place = jnp.where(lax.rem(member, 2) == 1, count - 1 - place, place)
    return jnp.where(lax.rem(member // 2, 2) == 1, lax.rem(place + count // 2, count), place)


def exchange_groups(count, members):
    ends = [x for pair in zip(range(count // 2), range(count - 1, count // 2 - 1, -1), strict=True) for x in pair]
    groups = []
    for member in range(members):
        order = ends[::-1] if member % 2 else ends
        if member // 2 % 2:
            order = order[count // 2 :] + order[: count // 2]
        if (members, count) == (len(ORDERS), len(ORDERS[0])):
            order = ORDERS[member]
        groups.append([device * members + member for device in order])
    return groups


def pack_kernel(basin_local, *refs):
    count = len(refs) // 2 - 1
    sources, send, held, semaphores = refs[:count], refs[count], refs[count + 1 : -1], refs[-1]
    copies = [
        pltpu.make_async_copy(source, target, semaphores.at[i])
        for i, (source, target) in enumerate(zip(sources, held, strict=True))
    ]
    for copy in copies:
        copy.start()
    for copy in copies:
        copy.wait()
    forcing, weight, part, slot, flow = held
    tile_local, members, width = forcing.shape
    groups = send.shape[0] // members
    half = tile_local // 2

    def pieces(values):
        high = values.astype(jnp.bfloat16).astype(jnp.float32)
        rest = values - high
        middle = rest.astype(jnp.bfloat16).astype(jnp.float32)
        return [high, middle, rest - middle]

    def side_by_side(rows):
        return jnp.concatenate([rows[entry : entry + 1] for entry in range(TOP)], axis=1)

    common = pieces(side_by_side(weight[...]))
    common += [side_by_side(part[...].astype(jnp.float32)), side_by_side(slot[...].astype(jnp.float32))]
    owners = LANES // basin_local
    lane = lax.broadcasted_iota(jnp.int32, (1, LANES), 1)
    mine = lane // basin_local == lax.rem(lax.axis_index("basin"), owners)
    mine_member = lax.axis_index("member")
    for member in range(members):
        tiles = forcing[:, member, :]
        first = tiles[:, :LANES]
        second = jnp.concatenate([tiles[:half, LANES:], tiles[half:, LANES:]], axis=1)
        own_flow = flow[member : member + 1, :]
        own_flow = jnp.concatenate([own_flow] * owners, axis=1)
        rows = common + pieces(jnp.where(mine, own_flow, 0.0))
        extras = jnp.concatenate(rows, axis=0).astype(jnp.bfloat16)
        for group in range(groups):
            place = position(member * groups + group, mine_member, send.shape[0])
            send[place, :tile_local, :] = first
            send[place, tile_local : tile_local + half, :] = second
            send[place, tile_local + half :, :] = extras


def encode(values):
    spread = values * (2.0**13 + 1.0)
    rounded = spread - (spread - values)
    place = (values - rounded) / jnp.maximum(rounded, 1e-30)
    digits = jnp.clip(jnp.floor(place * (1.5 * HALF_STEP) + 0.5), -1.0, 1.0)
    total = digits[0:1]
    for k in range(1, values.shape[0]):
        total = total + 3.0**k * digits[k : k + 1]
    return jnp.concatenate([rounded, total], axis=0)


def decode(rows):
    *rounded, total = rows
    values = []
    for row in rounded:
        above = jnp.floor(total * (1.0 / 3.0) + 0.5)
        values.append(row + row * ((total - 3.0 * above) * (1.0 / (1.5 * HALF_STEP))))
        total = above
    return values


def lstm_kernel(
    shape, arrived, small, w_encoder, w_decoder, out
):
    hour_feat, tile_local, basin_local, groups, sources = shape
    hours = hour_feat // FEAT
    devices = arrived.shape[0]
    rows = out.shape[1]
    units = w_encoder.shape[0]
    half = lax.rem(lax.axis_index("basin"), groups)
    first = (half * rows).astype(jnp.float32)
    folded = tile_local // 2
    extra_at = tile_local + folded

    def add_sources(chunk, total):
        block = arrived[pl.ds(chunk * sources, sources)].astype(jnp.float32)
        extras = block[:, extra_at:, :]
        weight = extras[:, 0] + extras[:, 1] + extras[:, 2]
        basin = extras[:, 3] * basin_local + extras[:, 4] - first
        weight = weight.T
        row_of = lax.broadcasted_iota(jnp.int32, (rows, TOP * tile_local), 0).astype(jnp.float32)
        picked, terms = [], []
        for source in range(sources):
            picked.append(jnp.where(row_of == basin[source : source + 1], 1.0, 0.0).astype(jnp.bfloat16))
            second = block[source, tile_local:extra_at, :]
            second = jnp.concatenate([second, pltpu.roll(second, LANES // 2, 1)], axis=0)
            tiles = jnp.concatenate([block[source, :tile_local, :], second], axis=1)
            for entry in range(TOP):
                column = weight[entry * tile_local : (entry + 1) * tile_local, source : source + 1]
                terms.append((column * tiles).astype(jnp.bfloat16))
        return total + dot(jnp.concatenate(picked, axis=1), jnp.concatenate(terms, axis=0))

    total = jnp.zeros((rows, 2 * LANES), jnp.float32)
    if devices == sources:
        total = add_sources(0, total)
    else:
        total = lax.fori_loop(0, devices // sources, add_sources, total)
    inputs = total.astype(jnp.bfloat16)

    owners = rows // basin_local
    member = lax.axis_index("member")
    flow = jnp.zeros((EXTRAS, rows), jnp.float32)
    for owner in range(owners):
        place = position(half * owners + owner, member, devices)
        flow = flow + arrived[place, extra_at:, :].astype(jnp.float32)
    results = []
    b_encoder, b_decoder = small[0:1, : 4 * units], small[1:2, : 4 * units]
    w_input = small[INPUT_ROW : INPUT_ROW + FEAT, : 4 * units].astype(jnp.bfloat16)
    w_output = jnp.broadcast_to(small[2:3, :units], (8, units)).astype(jnp.bfloat16)

    hidden = jnp.zeros((rows, units), jnp.bfloat16)
    memory_cell = jnp.zeros((rows, units), jnp.float32)
    ahead = dot(inputs[:, :FEAT], w_input) + b_encoder
    for hour in range(hours):
        gate_sum = ahead + dot(hidden, w_encoder[...]) if hour else ahead
        if hour + 1 < hours:
            ahead = dot(inputs[:, (hour + 1) * FEAT : (hour + 2) * FEAT], w_input) + b_encoder
        hidden, memory_cell = cell_update(gate_sum, memory_cell)

    def runoff(state):
        sums = lax.dot_general(
            w_output, state, (((1,), (1,)), ((), ())), preferred_element_type=jnp.float32
        )[0:1]
        return jnp.maximum(sums, 0.0) + jnp.log(1.0 + jnp.exp(-jnp.abs(sums)))

    for hour in range(DEC):
        gate_sum = dot(hidden, w_decoder[...]) + b_decoder
        if hour:
            results.append(runoff(hidden))
        hidden, memory_cell = cell_update(gate_sum, memory_cell)
    results.append(runoff(hidden))
    results.append(flow[5:6] + flow[6:7] + flow[7:8])
    out[...] = encode(jnp.concatenate(results, axis=0))


def power(flow):
    return jnp.exp(BETA * jnp.log(flow))


def route_kernel(member_local, basin_local, reaches, gathered, small, discharge, ensemble):
    celerity, storage, level_row = small[3:4, :reaches], small[4:5, :reaches], small[5:6, :reaches]
    upstream = small[6:10, :reaches]
    halves = reaches // LANES
    per_member = halves * 8
    members = gathered.shape[0] // per_member
    shape = (members, LANES)

    def spread(row):
        return [jnp.broadcast_to(row[:, h * LANES : (h + 1) * LANES], shape) for h in range(halves)]

    def pick(parts, index):
        out = None
        for h, part in enumerate(parts):
            value = jnp.take_along_axis(part, index & (LANES - 1), axis=1)
            out = value if out is None else jnp.where(index >= h * LANES, value, out)
        return out

    level_parts = spread(level_row.astype(jnp.int32))
    levels = jnp.concatenate(level_parts, axis=1)
    sources, lags = [], []
    for entry in range(upstream.shape[0]):
        named = spread(upstream[entry : entry + 1, :].astype(jnp.int32))
        index = [jnp.maximum(x, 0) for x in named]
        sources.append(index)
        lags.append(
            [jnp.where(x < 0, 0, level - pick(level_parts, i)) for x, level, i in zip(named, level_parts, index, strict=True)]
        )

    def handed_on(flow):
        parts = [flow[:, h * LANES : (h + 1) * LANES] for h in range(halves)]
        sums = [[jnp.zeros(shape, jnp.float32)] * halves for _ in range(LEVELS - 1)]
        for index, lag in zip(sources, lags, strict=True):
            for h in range(halves):
                value = pick(parts, index[h])
                for k in range(LEVELS - 1):
                    sums[k][h] = sums[k][h] + jnp.where(lag[h] == k + 1, value, 0.0)
        return [jnp.concatenate(x, axis=1) for x in sums]

    speed_rate = jnp.broadcast_to(celerity, (members, reaches))
    store_rate = jnp.broadcast_to(storage, (members, reaches))

    def row(k):
        return jnp.concatenate(
            [gathered[pl.ds(h * 8 + k, members, stride=per_member), :] for h in range(halves)], axis=1
        )

    *lateral, current = decode([row(k) for k in range(8)])
    powered = power(current)
    series = [jnp.zeros((members, reaches), jnp.float32) for _ in range(DEC)]
    given = []
    for step in range(DEC + LEVELS - 1):
        target = store_rate * powered
        for level in range(LEVELS):
            hour = step - level
            if 0 <= hour < DEC:
                target = jnp.where(levels == level, target + lateral[hour], target)
        for k in range(LEVELS - 1):
            if step - 1 - k >= 0:
                target = target + speed_rate * given[step - 1 - k][k]
        flow, flow_power = current, powered
        for _ in range(NEWTON):
            slope = speed_rate * flow + BETA * store_rate * flow_power
            reached = jnp.maximum(target - (1.0 - BETA) * store_rate * flow_power, 0.5 * slope)
            flow = flow * (reached / slope)
            flow_power = flow_power * jnp.exp(BETA * (jnp.log(reached) - jnp.log(slope)))
        active = (levels <= step) & (levels > step - DEC)
        current = jnp.where(active, flow, current)
        powered = jnp.where(active, flow_power, powered)
        given.append(handed_on(current) if step + 1 < DEC + LEVELS - 1 else None)
        for level in range(LEVELS):
            hour = step - level
            if 0 <= hour < DEC:
                series[hour] = jnp.where(levels == level, flow, series[hour])
    column = lax.axis_index("basin") * basin_local
    mine = lax.axis_index("member")
    block = column // LANES
    shift = lax.rem(LANES - lax.rem(column, LANES), LANES)
    for hour in range(DEC):
        value = series[hour]
        picked = value[:, 0:LANES]
        for h in range(1, halves):
            picked = jnp.where(block == h, value[:, h * LANES : (h + 1) * LANES], picked)
        picked = pltpu.roll(picked, shift, 1)
        kept = picked[0:member_local]
        for q in range(1, members // member_local):
            kept = jnp.where(mine == q, picked[q * member_local : (q + 1) * member_local], kept)
        discharge[hour] = kept[:, 0:basin_local]
        mean = jnp.sum(picked, axis=0, keepdims=True) / members
        ensemble[hour : hour + 1, :] = mean[:, 0:basin_local]


def route_plain(gathered, upstream, reach_level, celerity, storage, mem_local, basin_local):
    reaches = reach_level.shape[0]
    members = gathered.shape[0] * gathered.shape[2] // reaches
    whole = gathered.reshape(members, -1, gathered.shape[1], gathered.shape[2])
    whole = jnp.transpose(whole, (1, 3, 0, 2)).reshape(reaches, members, gathered.shape[1])
    *lateral, initial = decode([whole[:, :, k] for k in range(8)])
    lateral = jnp.stack(lateral, axis=2)
    speed_rate, store_rate = celerity[:, None], storage[:, None]
    up_index = jnp.where(upstream < 0, reaches, upstream)
    outflow = jnp.zeros_like(lateral)
    for level_now in range(LEVELS):
        padded = jnp.concatenate([outflow, jnp.zeros_like(outflow[:1])], axis=0)
        inflow = padded[up_index[:, 0]]
        for entry in range(1, up_index.shape[1]):
            inflow = inflow + padded[up_index[:, entry]]
        flow = initial
        hours = []
        for hour in range(DEC):
            flow_power = flow**BETA
            target = speed_rate * inflow[:, :, hour] + store_rate * flow_power + lateral[:, :, hour]
            for _ in range(NEWTON):
                flow_power = flow**BETA
                ratio = (target - (1.0 - BETA) * store_rate * flow_power) / (
                    speed_rate * flow + BETA * store_rate * flow_power
                )
                flow = flow * jnp.maximum(ratio, 0.5)
            hours.append(flow)
        routed = jnp.stack(hours, axis=2)
        outflow = jnp.where((reach_level == level_now)[:, None, None], routed, outflow)
    ensemble = jnp.sum(outflow, axis=1) / members
    first_row = lax.axis_index("basin") * basin_local
    mine = lax.dynamic_slice_in_dim(outflow, first_row, basin_local, 0)
    mine = lax.dynamic_slice_in_dim(mine, lax.axis_index("member") * mem_local, mem_local, 1)
    return mine, lax.dynamic_slice_in_dim(ensemble, first_row, basin_local, 0)


def on_device(
    forcing,
    tile_part,
    tile_slot,
    tile_weight,
    w_input,
    w_encoder,
    b_encoder,
    w_decoder,
    b_decoder,
    w_output,
    celerity,
    storage,
    initial_flow,
    reach_level,
    upstream,
):
    tile_local, mem_local, hour_feat = forcing.shape
    part_count = lax.axis_size("basin")
    basin_local = initial_flow.shape[0]
    reaches = reach_level.shape[0]
    groups = part_count // mem_local
    rows = reaches // groups
    in_kernel = reaches <= KERNEL_REACHES and rows == LANES
    tables = (celerity[None], storage[None], reach_level[None], upstream.T) if in_kernel else ()

    vmem = pl.BlockSpec(memory_space=pltpu.VMEM)
    params = pltpu.CompilerParams(vmem_limit_bytes=48 << 20)
    operands = (forcing, tile_weight.T, tile_part.T, tile_slot.T, initial_flow.T)
    send = pl.pallas_call(
        functools.partial(pack_kernel, basin_local),
        out_shape=jax.ShapeDtypeStruct(
            (part_count, tile_local + tile_local // 2 + EXTRAS, LANES), jnp.bfloat16
        ),
        in_specs=[pl.BlockSpec(memory_space=pltpu.HBM)] * len(operands),
        out_specs=vmem,
        scratch_shapes=[pltpu.VMEM(x.shape, x.dtype) for x in operands]
        + [pltpu.SemaphoreType.DMA((len(operands),))],
        compiler_params=pltpu.CompilerParams(vmem_limit_bytes=60 << 20),
    )(*operands)
    arrived = lax.all_to_all(
        send,
        ("basin", "member"),
        split_axis=0,
        concat_axis=0,
        tiled=True,
        axis_index_groups=exchange_groups(part_count, lax.axis_size("member")),
    )
    sources = min(part_count, 8)
    units = w_encoder.shape[0]
    scale = jnp.where(jnp.arange(4 * units) // units == 2, 1.0, 0.5).astype(jnp.float32)
    shared = (b_encoder[None] * scale, b_decoder[None] * scale, w_output[None], *tables)
    blank = jnp.zeros((INPUT_ROW - sum(x.shape[0] for x in shared), 1), jnp.float32)
    small = stacked(INPUT_ROW + FEAT, 4 * units, (*shared, blank, w_input * scale))
    w_encoder = (w_encoder * scale).astype(jnp.bfloat16)
    w_decoder = (w_decoder * scale).astype(jnp.bfloat16)
    lateral = pl.pallas_call(
        functools.partial(lstm_kernel, (hour_feat, tile_local, basin_local, groups, sources)),
        out_shape=jax.ShapeDtypeStruct((8, rows), jnp.float32),
        in_specs=[vmem] * 4,
        out_specs=vmem,
        compiler_params=params,
    )(arrived, small, w_encoder, w_decoder)
    axes = ("member", "basin")
    world = lax.axis_size("member") * part_count
    copies = jnp.broadcast_to(lateral.astype(CARRIED)[None], (world,) + lateral.shape)
    gathered = lax.all_to_all(copies, axes, split_axis=0, concat_axis=0, tiled=True)
    gathered = gathered.astype(jnp.float32)
    if not in_kernel:
        return route_plain(gathered, upstream, reach_level, celerity, storage, mem_local, basin_local)
    discharge, ensemble = pl.pallas_call(
        functools.partial(route_kernel, mem_local, basin_local, reaches),
        out_shape=(
            jax.ShapeDtypeStruct((DEC, mem_local, basin_local), jnp.float32),
            jax.ShapeDtypeStruct((DEC, basin_local), jnp.float32),
        ),
        in_specs=[vmem] * 2,
        out_specs=(vmem, vmem),
        compiler_params=params,
    )(gathered.reshape(world * 8, rows), small)
    return jnp.transpose(discharge, (2, 1, 0)), ensemble.T


def solution(mesh):
    placed = (
        P("basin", "member", None),
        P("basin", None),
        P("basin", None),
        P("basin", None),
        P(),
        P(),
        P(),
        P(),
        P(),
        P(),
        P(),
        P(),
        P("basin", "member"),
        P(),
        P(),
    )
    return jax.shard_map(
        on_device,
        mesh=mesh,
        in_specs=placed,
        out_specs=(P("basin", "member", None), P("basin", None)),
        check_vma=False,
    )
```
